256 devices in a mesh: gx: 16 (over y_hi, x, core), gy: 16 (over y_lo, z).
Axes of the slice: x: 4, y: 4 (y_hi: 2, y_lo: 2; y = y_hi * 2 + y_lo), z: 8, core: 2. Of those that a mesh axis runs over, the one named last changes fastest.
Arguments:
- velocity: bfloat16 [4, 2, 256, 2048], P(None, None, 'gy', 'gx'), may hold values from -6 to 6
- conv_one: bfloat16 [2, 5, 5, 128], replicated, may hold values from -0.875 to 0.875
- bias_one: float32 [128], replicated, may hold values from -3 to 3
- conv_two: bfloat16 [5, 5, 64, 128], replicated, may hold values from -0.109375 to 0.109375
- bias_two: float32 [64], replicated, may hold values from -3 to 3
- conv_three: bfloat16 [2, 3, 3, 64], replicated, may hold values from -0.25 to 0.25
- bias_three: float32 [2], replicated, may hold values from -3 to 3
- drop_one: int32 [2, 128], replicated, may hold values 0 or 1
- drop_two: int32 [2, 64], replicated, may hold values 0 or 1
- thickness: float32 [4], replicated, may hold values from 0.5 to 2
- eta_old: float32 [256, 2048], P('gy', 'gx'), may hold values from -6 to 6
- face_coef: float32 [2, 256, 2048], P(None, 'gy', 'gx'), may hold values from 0.5 to 5
- storage: float32 [256, 2048], P('gy', 'gx'), may hold values from 0.05 to 0.5
- ocean: int32 [256, 2048], P('gy', 'gx'), may hold values 0 or 1
Outputs:
- forcing: float32 [4, 2, 256, 2048], P(None, None, 'gy', 'gx')
- eta_new: float32 [256, 2048], P('gy', 'gx')
The draws below stay inside these ranges and needn't reach their ends.
Inputs may be any that keep to these rules, and one draw needn't show every extreme that they name: 1 marks an ocean column, 0 land. `drop_one`: 1 keeps a channel, 0 drops it. `drop_two`: 1 keeps a channel, 0 drops it.
All inputs are finite; a program needn't handle non-finite values. No bound on the sum of `ocean` on one device may be relied on, other than what follows from the above.
Results may differ from the reference program's by a relative error of at most 0.0056.
Values may be sent and summed in bfloat16 or wider, within the bound.
A program may use at most 64 MiB of HBM per device.

```python
import math
import jax
import jax.numpy as jnp
from jax import lax

LEVELS = 4
MASKS = 2
CH1 = 128
CH2 = 64
K_WIDE = 5
K_NARROW = 3
ITERS = 3
NLAT = 256
NLON = 2048


def set_ends(array, own_key, smallest, high):
    longest = array.shape.index(max(array.shape))
    spots = []
    for shift in (0, 1):
        where = [jax.random.randint(jax.random.fold_in(own_key, axis), (), 0, length) for axis, length in enumerate(array.shape)]
        where[longest] = (where[longest] + shift) % array.shape[longest]
        spots.append(tuple(where))
    return array.at[spots[0]].set(smallest).at[spots[1]].set(high)


def shard_levels(key, extent, cuts, low, top_value):
    gain = 1.0
    for position, parts in cuts:
        steps = jax.random.uniform(jax.random.fold_in(jax.random.fold_in(key, 6), position), (parts,), jnp.float32, low / len(cuts), top_value / len(cuts))
        gain = gain * jnp.repeat(jnp.exp(steps), extent[position] // parts).reshape((-1,) + (1,) * (len(extent) - 1 - position))
    return gain


def bell_draw(rng, shape, spread, most, cuts=(), kind=jnp.bfloat16):
    entries = jax.random.normal(rng, shape, jnp.float32) * spread
    if len(cuts) > 0:
        entries = shard_levels(rng, shape, cuts, -0.22, 0.18) * entries
    return jnp.clip(entries, min=-most, max=most).astype(kind)


def setup_inputs(seed: int = 0) -> dict:
    arg_keys = jax.random.split(jax.random.key(seed), 15)
    velocity = bell_draw(arg_keys[0], (LEVELS, 2, NLAT, NLON), 1.0, 6.0, ((2, 16), (3, 16)))
    conv_one = bell_draw(arg_keys[1], (2, K_WIDE, K_WIDE, CH1), (2 * K_WIDE * K_WIDE) ** -0.5, 0.875)
    bias_one = bell_draw(arg_keys[2], (CH1,), 0.5, 3.0, (), jnp.float32)
    conv_two = bell_draw(arg_keys[3], (K_WIDE, K_WIDE, CH2, CH1), (CH1 * K_WIDE * K_WIDE) ** -0.5, 0.109375)
    bias_two = bell_draw(arg_keys[4], (CH2,), 0.5, 3.0, (), jnp.float32)
    conv_three = bell_draw(arg_keys[5], (2, K_NARROW, K_NARROW, CH2), (CH2 * K_NARROW * K_NARROW) ** -0.5, 0.25)
    bias_three = bell_draw(arg_keys[6], (2,), 0.5, 3.0, (), jnp.float32)
    drop_one = set_ends((jax.random.randint(arg_keys[7], (MASKS, CH1), 0, 4) < 3).astype(jnp.int32), jax.random.fold_in(arg_keys[7], 1), 0, 1)
    drop_two = set_ends((jax.random.randint(arg_keys[8], (MASKS, CH2), 0, 4) < 3).astype(jnp.int32), jax.random.fold_in(arg_keys[8], 1), 0, 1)
    thickness = jnp.clip(jnp.exp(jax.random.uniform(arg_keys[9], (LEVELS,), jnp.float32, math.log(0.5), math.log(2.0))), 0.5, 2.0)
    eta_old = bell_draw(arg_keys[10], (NLAT, NLON), 1.0, 6.0, ((0, 16), (1, 16)), jnp.float32)
    face_coef = jnp.clip(jnp.exp(math.log(5.0) - 2.3025851 * jax.random.uniform(arg_keys[11], (2, NLAT, NLON), jnp.float32) ** shard_levels(arg_keys[11], (2, NLAT, NLON), ((1, 16), (2, 16)), -0.2, 0.2)), 0.5, 5.0)
    storage = jnp.clip(jnp.exp(math.log(0.5) - 2.3025851 * jax.random.uniform(arg_keys[12], (NLAT, NLON), jnp.float32) ** shard_levels(arg_keys[12], (NLAT, NLON), ((0, 16), (1, 16)), -0.2, 0.2)), 0.05, 0.5)
    ocean = set_ends((jax.random.randint(arg_keys[13], (NLAT, NLON), 0, 8) < 7).astype(jnp.int32), jax.random.fold_in(arg_keys[13], 1), 0, 1)
    return {"velocity": velocity, "conv_one": conv_one, "bias_one": bias_one, "conv_two": conv_two, "bias_two": bias_two, "conv_three": conv_three, "bias_three": bias_three, "drop_one": drop_one, "drop_two": drop_two, "thickness": thickness, "eta_old": eta_old, "face_coef": face_coef, "storage": storage, "ocean": ocean}


keep_rate = 0.75


def pad_grid(field, width):
    wrapped = jnp.concatenate([field[..., -width:], field, field[..., :width]], axis=-1)
    spec = [(0, 0)] * (field.ndim - 2) + [(width, width), (0, 0)]
    return jnp.pad(wrapped, spec)


def convolve(field, kernel, layout):
    return lax.conv_general_dilated(field, kernel, (1, 1), "VALID", dimension_numbers=("NCHW", layout, "NCHW"), preferred_element_type=jnp.float32)


def neighbours(padded):
    return padded[1:-1, 2:], padded[1:-1, :-2], padded[2:, 1:-1], padded[:-2, 1:-1]


def reference(velocity, conv_one, bias_one, conv_two, bias_two, conv_three, bias_three, drop_one, drop_two, thickness, eta_old, face_coef, storage, ocean):
    keep_first = drop_one.astype(jnp.float32) / keep_rate
    keep_second = drop_two.astype(jnp.float32) / keep_rate

    def sample(index):
        mask_index = index // LEVELS
        level = index % LEVELS
        field = lax.dynamic_index_in_dim(velocity, level, 0, keepdims=True)
        scale_one = lax.dynamic_index_in_dim(keep_first, mask_index, 0, keepdims=False)
        scale_two = lax.dynamic_index_in_dim(keep_second, mask_index, 0, keepdims=False)
        first = convolve(pad_grid(field, K_WIDE // 2), conv_one, "IHWO") + bias_one[None, :, None, None]
        hidden_one = (jax.nn.relu(first) * scale_one[None, :, None, None]).astype(jnp.bfloat16)
        second = convolve(pad_grid(hidden_one, K_WIDE // 2), conv_two, "HWOI") + bias_two[None, :, None, None]
        hidden_two = (jax.nn.relu(second) * scale_two[None, :, None, None]).astype(jnp.bfloat16)
        return (convolve(pad_grid(hidden_two, K_NARROW // 2), conv_three, "OHWI") + bias_three[None, :, None, None])[0]

    outputs = lax.map(sample, jnp.arange(MASKS * LEVELS, dtype=jnp.int32))
    forcing = jnp.sum(outputs.reshape(MASKS, LEVELS, 2, NLAT, NLON), axis=0) / MASKS

    moved = velocity.astype(jnp.float32) + forcing
    zonal = jnp.sum(thickness[:, None, None] * moved[:, 0], axis=0)
    merid = jnp.sum(thickness[:, None, None] * moved[:, 1], axis=0)
    sea_here = ocean.astype(jnp.float32)
    sea_east, sea_west, sea_north, sea_south = neighbours(pad_grid(sea_here, 1))
    open_east = sea_here * sea_east
    open_west = sea_here * sea_west
    open_north = sea_here * sea_north
    open_south = sea_here * sea_south
    face_pad = pad_grid(face_coef, 1)
    coef_east = face_coef[0] * open_east
    coef_west = face_pad[0, 1:-1, :-2] * open_west
    coef_north = face_coef[1] * open_north
    coef_south = face_pad[1, :-2, 1:-1] * open_south
    flux = jnp.stack([zonal * open_east, merid * open_north])
    flux_pad = pad_grid(flux, 1)
    diverge = flux[0] - flux_pad[0, 1:-1, :-2] + flux[1] - flux_pad[1, :-2, 1:-1]
    right = storage * eta_old - diverge

    def operate(field):
        to_east, to_west, to_north, to_south = neighbours(pad_grid(field, 1))
        return storage * field + coef_east * (field - to_east) + coef_west * (field - to_west) + coef_north * (field - to_north) + coef_south * (field - to_south)

    solution = eta_old
    residual = right - operate(eta_old)
    direction = residual
    norm_now = jnp.sum(residual * residual)
    for number in range(ITERS):
        image = operate(direction)
        alpha = norm_now / jnp.sum(direction * image)
        solution = solution + alpha * direction
        residual = residual - alpha * image
        norm_next = jnp.sum(residual * residual)
        direction = residual + (norm_next / norm_now) * direction
        norm_now = norm_next
    return forcing, solution
```

```python
import functools

import jax
import jax.numpy as jnp
from jax import lax
from jax.experimental import pallas as pl
from jax.experimental.pallas import tpu as pltpu
from jax.sharding import PartitionSpec as P

MESH = pl.DeviceIdType.MESH
F32 = jnp.float32
BF16 = jnp.bfloat16
KEEP_SCALE = 4.0 / 3.0

WAYS = ((1, 0), (-1, 0), (0, 1), (0, -1), (1, 1), (-1, 1), (1, -1), (-1, -1))

ROWS, COLS, LEVELS = 16, 128, 4
XO_V, XO_1, XO_2 = 42, 38, 34
M_V, M_1, M_2 = 16 * XO_V, 16 * XO_1, 16 * XO_2


def iota(shape, dim):
    return lax.broadcasted_iota(jnp.int32, shape, dim)


def dot_t(a, b):
    return lax.dot_general(a, b, (((1,), (1,)), ((), ())), preferred_element_type=F32)


def dot(a, b):
    return jnp.dot(a, b, preferred_element_type=F32)


def shift_lanes(x, by):
    return pltpu.roll(x, by % x.shape[1], 1)


def shift_rows(x, by):
    return pltpu.roll(x, by % x.shape[0], 0)


def kernel(
    nx,
    ny,
    vel,
    w1,
    b1,
    w2,
    b2,
    w3,
    b3,
    d1,
    d2,
    thick,
    eta,
    face,
    stor,
    ocean,
    f_out,
    e_out,
    v_rows,
    v_cols,
    v_corner,
    st_own,
    fx_own,
    rv_rows,
    rv_cols,
    rv_corner,
    rst_cols,
    rst_rows,
    rfx_cols,
    rfx_rows,
    red_a,
    red_b,
    got_a,
    got_b,
    vx,
    bmat,
    pick,
    umat,
    w1pad,
    w1all,
    w2all,
    w3f,
    h1,
    zacc,
    perm,
    v_send,
    v_recv,
    s_send,
    s_recv,
    x_send,
    x_recv,
    a_send,
    a_recv,
    b_send,
    b_recv,
):
    mx = lax.axis_index("gx")
    my = lax.axis_index("gy")

    def there(step_x, step_y):
        return (lax.rem(mx + step_x + nx, nx), lax.rem(my + step_y + ny, ny))

    barrier = pltpu.get_barrier_semaphore()
    peers = [there(k, 0) for k in range(1, nx)]
    peers += [there(0, k) for k in range(1, ny)]
    peers += [there(sx, sy) for sx, sy in WAYS[4:]]
    for peer in peers:
        pl.semaphore_signal(barrier, inc=1, device_id=peer, device_id_type=MESH)

    lane = iota((ROWS, COLS), 1)
    group = lane // 32
    low = lane % 32 < 16
    own = [[vel[l, c].astype(F32) for c in range(2)] for l in range(LEVELS)]
    for c in range(2):
        packed = None
        for l in range(LEVELS):
            first = own[l][c] if l == 0 else shift_lanes(own[l][c], 32 * l)
            last = own[l][c] if l == 3 else shift_lanes(own[l][c], 32 * (l + 1))
            both = jnp.where(low, first, last)
            packed = both if l == 0 else jnp.where(group == l, both, packed)
        v_cols[pl.ds(16 * c, 16), :] = packed.astype(BF16)
        if c == 0:
            packed_first = packed
    for side in range(2):
        cut = slice(8, 16) if side == 0 else slice(0, 8)
        rows = jnp.concatenate([own[l][c][cut] for l in range(LEVELS) for c in range(2)], axis=0)
        v_rows[side] = rows.astype(BF16)
        v_corner[side] = jnp.concatenate([packed_first[cut], packed[cut]], axis=0).astype(BF16)
    st_own[0] = eta[...]
    st_own[1] = face[0]
    st_own[2] = face[1]
    st_own[3] = stor[...]
    st_own[4] = ocean[...].astype(F32)

    pl.semaphore_wait(barrier, len(peers))

    copies_v, copies_s = [], []
    for d, (sx, sy) in enumerate(WAYS):
        side = 0 if sy == 1 else 1
        if sy == 0:
            src, dst = v_cols, rv_cols.at[d]
        elif sx == 0:
            src, dst = v_rows.at[side], rv_rows.at[d - 2]
        else:
            src, dst = v_corner.at[side], rv_corner.at[d - 4]
        copy = pltpu.make_async_remote_copy(
            src_ref=src,
            dst_ref=dst,
            send_sem=v_send.at[d],
            recv_sem=v_recv.at[d],
            device_id=there(sx, sy),
            device_id_type=MESH,
        )
        copy.start()
        copies_v.append(copy)
    for d, (sx, sy) in enumerate(WAYS):
        if sy == 0:
            src, dst = st_own, rst_cols.at[d]
        else:
            src = st_own.at[:, pl.ds(8 if sy == 1 else 0, 8), :]
            dst = rst_rows.at[d - 2]
        copy = pltpu.make_async_remote_copy(
            src_ref=src,
            dst_ref=dst,
            send_sem=s_send.at[d],
            recv_sem=s_recv.at[d],
            device_id=there(sx, sy),
            device_id_type=MESH,
        )
        copy.start()
        copies_s.append(copy)

    w1pad[...] = jnp.zeros_like(w1pad)
    for c in range(2):
        for dy in range(5):
            taps = w1[c, dy].astype(F32)
            for dx in range(5):
                w1pad[dx, c, pl.ds(10 + dy, 1), pl.ds(0, 128)] = taps[dx : dx + 1]
                w1pad[dx, c, pl.ds(11 + dy, 1), pl.ds(128, 128)] = taps[dx : dx + 1]
    for s in range(6):
        for dx in range(5):
            for c in range(2):
                block = w1pad[dx, c, pl.ds(10 - 2 * s, 16), :]
                w1all[s, pl.ds(32 * dx + 16 * c, 16), :] = block.astype(BF16)
        w1all[s, pl.ds(160, 96), :] = jnp.zeros((96, 256), BF16)

    kept = [d1[pl.ds(m, 1), :].astype(F32).astype(BF16) for m in range(2)]
    nothing = jnp.zeros((64, 128), BF16)
    for dx in range(5):
        for dy in range(-1, 6):
            for m in range(2):
                block = w2[dy, dx] * kept[m] if 0 <= dy < 5 else nothing
                for b in range(2):
                    if 0 <= dy + b < 6:
                        o, a = divmod(dy + b, 2)
                        w2all[pl.ds(128 * b + 64 * m, 64), pl.ds(((o * 5 + dx) * 2 + a) * 128, 128)] = block

    w3f[...] = jnp.zeros_like(w3f)
    for c in range(2):
        for ky in range(3):
            taps = w3[c, ky].astype(F32) * 0.5
            for dx in range(3):
                tap = taps[dx : dx + 1]
                both = jnp.concatenate([tap, tap], axis=1)
                for b in range(2):
                    w3f[pl.ds(8 * dx + 4 * c + b + 2 - ky, 1), pl.ds(128 * b, 128)] = both

    r = iota((M_V, 128), 0)
    lev = (r // 4) % 4
    x = 32 * (r % 4) + r // 16 - 5
    spot = jnp.where(x < 0, 512 + 32 * lev + 32 + x, jnp.where(x < 128, 128 * lev + x, 384 + 32 * lev + x))
    for k in range(5):
        pick[:, pl.ds(128 * k, 128)] = jnp.where(iota((M_V, 128), 1) + 128 * k == spot, 1.0, 0.0).astype(BF16)
    r = iota((512, 128), 0)
    spot = 128 * ((r // 4) % 4) + 32 * (r % 4) + r // 16
    for k in range(4):
        perm[:, pl.ds(128 * k, 128)] = jnp.where(iota((512, 128), 1) + 128 * k == spot, 1.0, 0.0).astype(BF16)

    has_south = jnp.where(my > 0, 1.0, 0.0)
    has_north = jnp.where(my < ny - 1, 1.0, 0.0)
    for copy in copies_v:
        copy.wait_recv()
    low8 = low[:8]
    south = rv_rows[0].astype(F32) * has_south
    north = rv_rows[1].astype(F32) * has_north
    from_w, from_e = rv_cols[0].astype(F32), rv_cols[1].astype(F32)
    from_sw, from_se = rv_corner[0].astype(F32), rv_corner[1].astype(F32)
    from_nw, from_ne = rv_corner[2].astype(F32), rv_corner[3].astype(F32)
    for c in range(2):
        for l in range(LEVELS):
            at = 8 * (2 * l + c)
            vx[l, c, pl.ds(0, 8), :] = south[at : at + 8]
            vx[l, c, pl.ds(8, 16), :] = own[l][c]
            vx[l, c, pl.ds(24, 8), :] = north[at : at + 8]
        cut = slice(8 * c, 8 * c + 8)
        vx[4, c, pl.ds(0, 8), :] = jnp.where(low8, from_se[cut], from_sw[cut]) * has_south
        cut16 = slice(16 * c, 16 * c + 16)
        vx[4, c, pl.ds(8, 16), :] = jnp.where(low, from_e[cut16], from_w[cut16])
        vx[4, c, pl.ds(24, 8), :] = jnp.where(low8, from_ne[cut], from_nw[cut]) * has_north
    for w in range(2):
        for k in range(5):
            for c in range(2):
                block = vx[k, c, pl.ds(3 + 10 * w, 16), :].astype(BF16)
                for rep in range(4):
                    bmat[pl.ds(128 * w + 32 * rep + 16 * c, 16), pl.ds(128 * k, 128)] = block
    umat[...] = dot_t(pick[...], bmat[...]).astype(BF16)

    bias1 = jnp.concatenate([b1[...].reshape(1, 128)] * 2, axis=1)
    upper = iota((1, 256), 1) // 128
    group1 = iota((M_1, 128), 1) // 32
    for w in range(2):
        lanes = pl.ds(128 * w, 128)
        near = umat[pl.ds(0, M_1), lanes]
        for g in range(1, 4):
            near = jnp.where(group1 == g, umat[pl.ds(16 * g, M_1), lanes], near)
        wide = jnp.concatenate([near, umat[pl.ds(64, M_1), lanes]], axis=1)

        def layer_one(j, carry, w=w, wide=wide):
            acc = dot(wide, w1all[j - 5 * w])
            row = my * ROWS + 2 * j - 3 + upper
            scale = jnp.where((row >= 0) & (row < ny * ROWS), KEEP_SCALE, 0.0)
            h1[j] = (jnp.maximum(acc + bias1, 0.0) * scale).astype(BF16)
            return carry

        lax.fori_loop(6 * w, 6 + 5 * w, layer_one, 0)

    bias2 = jnp.concatenate([b2[...].reshape(1, 64)] * 4, axis=1)
    keep2 = d2[...].astype(F32) * KEEP_SCALE
    keep2 = jnp.concatenate([keep2[0:1], keep2[1:2]] * 2, axis=1)
    zacc[...] = jnp.zeros_like(zacc)
    w3all = w3f[...].astype(BF16)

    def layer_two(n, carry):
        acc = None
        for o in range(3):
            for dx in range(5):
                left = h1[pl.ds(3 * n + o, 3), pl.ds(16 * dx, M_2), :].reshape(3 * M_2, 256)
                term = dot_t(left, w2all[:, pl.ds((o * 5 + dx) * 256, 256)])
                acc = term if acc is None else acc + term
        for q in range(3):
            i = 3 * n + q
            row = my * ROWS + 2 * i - 1 + upper
            scale = jnp.where((row >= 0) & (row < ny * ROWS), keep2, 0.0)
            hidden = (jnp.maximum(acc[M_2 * q : M_2 * (q + 1)] + bias2, 0.0) * scale).astype(BF16)
            z = dot_t(w3all, hidden)
            part = z[0:8, 0:512] + z[8:16, 16:528] + z[16:24, 32:544]
            for c in range(2):
                for t in range(4):
                    at = pl.ds(2 * i + t, 1)
                    zacc[c, at, :] = zacc[c, at, :] + part[4 * c + t : 4 * c + t + 1]
        return carry

    lax.fori_loop(0, 3, layer_two, 0)

    mixed = jnp.concatenate([zacc[0, pl.ds(2, 16), :], zacc[1, pl.ds(2, 16), :]], axis=0)
    high = mixed.astype(BF16)
    rest = (mixed - high.astype(F32)).astype(BF16)
    out = dot(jnp.concatenate([high, rest], axis=0), perm[...])
    out = out[0:32] + out[32:64]
    for c in range(2):
        total = None
        for l in range(LEVELS):
            forcing = out[16 * c : 16 * c + 16, 128 * l : 128 * l + 128] + b3[c]
            f_out[l, c] = forcing
            term = thick[l] * (vel[l, c].astype(F32) + forcing)
            total = term if total is None else total + term
        fx_own[c] = total

    copies_x = []
    for d, (sx, sy) in enumerate(WAYS):
        if sy == 0:
            src, dst = fx_own, rfx_cols.at[d]
        else:
            src = fx_own.at[:, pl.ds(8 if sy == 1 else 0, 8), :]
            dst = rfx_rows.at[d - 2]
        copy = pltpu.make_async_remote_copy(
            src_ref=src,
            dst_ref=dst,
            send_sem=x_send.at[d],
            recv_sem=x_recv.at[d],
            device_id=there(sx, sy),
            device_id_type=MESH,
        )
        copy.start()
        copies_x.append(copy)

    for copy in copies_s:
        copy.wait_recv()

    side = iota((ROWS, COLS), 1) < 64
    side8 = side[:8]

    def widened(own_ref, cols_ref, rows_ref, k):
        middle = jnp.concatenate([own_ref[k], jnp.where(side, cols_ref[1, k], cols_ref[0, k])], axis=1)
        below = jnp.concatenate([rows_ref[0, k], jnp.where(side8, rows_ref[3, k], rows_ref[2, k])], axis=1)
        above = jnp.concatenate([rows_ref[1, k], jnp.where(side8, rows_ref[5, k], rows_ref[4, k])], axis=1)
        return jnp.concatenate([below, middle, above], axis=0)

    eta_w, east_w, north_w, stor_w, sea = [widened(st_own, rst_cols, rst_rows, k) for k in range(5)]
    place = iota(sea.shape, 0) - 8 + my * ROWS
    sea = jnp.where((place >= 0) & (place < ny * ROWS), sea, 0.0)
    open_east = sea * shift_lanes(sea, -1)
    open_north = sea * shift_rows(sea, -1)
    coef_east = east_w * open_east
    coef_north = north_w * open_north
    coef_west = shift_lanes(coef_east, 1)
    coef_south = shift_rows(coef_north, 1)
    diagonal = stor_w + coef_east + coef_west + coef_north + coef_south

    def operate(field):
        return (
            diagonal * field
            - coef_east * shift_lanes(field, -1)
            - coef_west * shift_lanes(field, 1)
            - coef_north * shift_rows(field, -1)
            - coef_south * shift_rows(field, 1)
        )

    known = stor_w * eta_w - operate(eta_w)
    for copy in copies_x:
        copy.wait_recv()
    zonal, merid = [widened(fx_own, rfx_cols, rfx_rows, k) for k in range(2)]
    flux_east = zonal * open_east
    flux_north = merid * open_north
    diverge = flux_east - shift_lanes(flux_east, 1) + flux_north - shift_rows(flux_north, 1)
    k0 = known - diverge
    k1 = operate(k0)
    k2 = operate(k1)
    k3 = operate(k2)
    k0, k1, k2, k3 = [k[8:24, 0:128] for k in (k0, k1, k2, k3)]

    slot = iota((8, 128), 0)
    sums = jnp.zeros((8, 128), F32)
    for n, (a, b) in enumerate(((k0, k0), (k0, k1), (k1, k1), (k1, k2), (k2, k2), (k2, k3))):
        sums = jnp.where(slot == n, jnp.sum(a * b, axis=0, keepdims=True), sums)

    def exchange(values, mine, got, send, recv, count, target):
        mine[...] = values
        copies = []
        for k in range(1, count):
            copy = pltpu.make_async_remote_copy(
                src_ref=mine,
                dst_ref=got.at[k - 1],
                send_sem=send.at[k - 1],
                recv_sem=recv.at[k - 1],
                device_id=target(k),
                device_id_type=MESH,
            )
            copy.start()
            copies.append(copy)
        for copy in copies:
            copy.wait_recv()
        return values + jnp.sum(got[...], axis=0), copies

    sums, copies_a = exchange(sums, red_a, got_a, a_send, a_recv, nx, lambda k: there(k, 0))
    sums, copies_b = exchange(sums, red_b, got_b, b_send, b_recv, ny, lambda k: there(0, k))
    sums = jnp.sum(sums, axis=1, keepdims=True)
    m0, m1, m2, m3, m4, m5 = [jnp.broadcast_to(sums[n : n + 1], (1, 128)) for n in range(6)]

    def over(value, scale):
        fine = value > 1e-6 * scale
        return jnp.where(fine, 1.0 / jnp.where(fine, value, 1.0), 0.0)

    inv0 = over(m1, jnp.zeros_like(m1))
    l1 = m2 * inv0
    l2 = m3 * inv0
    p1 = m3 - l1 * m2
    inv1 = over(p1, m3)
    e21 = m4 - l2 * m2
    l21 = e21 * inv1
    p2 = m5 - l2 * m3 - l21 * e21
    inv2 = jnp.where(inv1 > 0.0, over(p2, m5), 0.0)
    z1 = m1 - l1 * m0
    z2 = m2 - l2 * m0 - l21 * z1
    c2 = z2 * inv2
    c1 = z1 * inv1 - l21 * c2
    c0 = m0 * inv0 - l1 * c1 - l2 * c2
    e_out[...] = eta[...] + c0 * k0 + c1 * k1 + c2 * k2

    for copy in copies_v + copies_s + copies_x + copies_a + copies_b:
        copy.wait_send()


def body(nx, ny, *args):
    vmem = pl.BlockSpec(memory_space=pltpu.VMEM)
    smem = pl.BlockSpec(memory_space=pltpu.SMEM)
    dma = pltpu.SemaphoreType.DMA
    V = pltpu.VMEM
    return pl.pallas_call(
        functools.partial(kernel, nx, ny),
        out_shape=(
            jax.ShapeDtypeStruct((LEVELS, 2, ROWS, COLS), F32),
            jax.ShapeDtypeStruct((ROWS, COLS), F32),
        ),
        in_specs=[vmem] * 6 + [smem] + [vmem] * 2 + [smem] + [vmem] * 4,
        out_specs=(vmem, vmem),
        scratch_shapes=[
            V((2, 64, 128), BF16),
            V((32, 128), BF16),
            V((2, 16, 128), BF16),
            V((5, ROWS, COLS), F32),
            V((2, ROWS, COLS), F32),
            V((2, 64, 128), BF16),
            V((2, 32, 128), BF16),
            V((4, 16, 128), BF16),
            V((2, 5, ROWS, COLS), F32),
            V((6, 5, 8, COLS), F32),
            V((2, 2, ROWS, COLS), F32),
            V((6, 2, 8, COLS), F32),
            V((8, 128), F32),
            V((8, 128), F32),
            V((nx - 1, 8, 128), F32),
            V((ny - 1, 8, 128), F32),
            V((5, 2, 32, 128), F32),
            V((256, 640), BF16),
            V((M_V, 640), BF16),
            V((M_V, 256), BF16),
            V((5, 2, 32, 256), F32),
            V((6, 256, 256), BF16),
            V((256, 3840), BF16),
            V((32, 256), F32),
            V((11, M_1, 256), BF16),
            V((2, 24, 512), F32),
            V((512, 512), BF16),
            dma((8,)),
            dma((8,)),
            dma((8,)),
            dma((8,)),
            dma((8,)),
            dma((8,)),
            dma((nx - 1,)),
            dma((nx - 1,)),
            dma((ny - 1,)),
            dma((ny - 1,)),
        ],
        compiler_params=pltpu.CompilerParams(
            collective_id=0, has_side_effects=True, vmem_limit_bytes=48 * 2**20
        ),
        name="ocean_step",
    )(*args)


def solution(mesh):
    nx, ny = mesh.shape["gx"], mesh.shape["gy"]
    tile = P("gy", "gx")
    stacked = P(None, "gy", "gx")
    levels = P(None, None, "gy", "gx")
    in_specs = (levels,) + (P(),) * 9 + (tile, stacked, tile, tile)
    return jax.shard_map(
        functools.partial(body, nx, ny),
        mesh=mesh,
        in_specs=in_specs,
        out_specs=(levels, tile),
        check_vma=False,
    )
```

```python
import functools
import itertools

import jax
import jax.numpy as jnp
from jax import lax
from jax.experimental import pallas as pl
from jax.experimental.pallas import tpu as pltpu
from jax.sharding import PartitionSpec as P

MESH = pl.DeviceIdType.MESH
F32 = jnp.float32
BF16 = jnp.bfloat16
KEEP_SCALE = 4.0 / 3.0

WAYS = ((1, 0), (-1, 0), (0, 1), (0, -1), (1, 1), (-1, 1), (1, -1), (-1, -1))

ROWS, COLS, LEVELS = 16, 128, 4
SEND_ORDER = (4, 5, 6, 7, 2, 3, 0, 1)

SPLIT_X = ((2, 2), (4, 1), (2, 0))
SPLIT_Y = ((2, 1), (8, 1))

LOAD_ORDER = (0, 10, 11, 12, 13, 1, 7, 3, 5, 2, 4, 6, 8, 9)

XO_V, XO_1, XO_2 = 42, 38, 34
EDGE_W, EDGE_E = 5, 28
M_V, M_1, M_2 = 16 * XO_V, 16 * XO_1, 16 * XO_2


def iota(shape, dim):
    return lax.broadcasted_iota(jnp.int32, shape, dim)


def dot_t(a, b):
    return lax.dot_general(a, b, (((1,), (1,)), ((), ())), preferred_element_type=F32)


def dot(a, b):
    return jnp.dot(a, b, preferred_element_type=F32)


def others(index, split):
    sizes = [size for size, _ in split]
    steps = list(itertools.product(*[range(size) for size in sizes]))[1:]
    steps.sort(key=lambda step: -sum(hops * min(k, size - k) for k, (size, hops) in zip(step, split)))
    found = []
    for step in steps:
        at, stride = 0, 1
        for k, size in reversed(list(zip(step, sizes))):
            digit = lax.rem(lax.div(index, jnp.int32(stride)), jnp.int32(size))
            at = at + lax.rem(digit + k, jnp.int32(size)) * stride
            stride *= size
        found.append(at)
    return found


def shift_lanes(x, by):
    return pltpu.roll(x, by % x.shape[1], 1)


def shift_rows(x, by):
    return pltpu.roll(x, by % x.shape[0], 0)


def kernel(
    nx,
    ny,
    *refs,
):
    given, refs = refs[:14], refs[14:]
    (f_out, e_out), refs = refs[:2], refs[2:]
    here, refs = refs[:14], refs[14:]
    vel, w1, b1, w2, b2, w3, b3, d1, d2, thick, eta, face, stor, ocean = here
    (
        v_rows,
        v_cols,
        v_corner,
        st_own,
        fx_own,
        fx_all,
        rv_rows,
        rv_cols,
        rv_corner,
        rst_cols,
        rst_rows,
        rfx_cols,
        rfx_rows,
        red_a,
        red_b,
        got_a,
        got_b,
        vx,
        bmat,
        pick,
        umat,
        w1pad,
        w1all,
        w2all,
        w3f,
        h1,
        h2,
        zacc,
        perm,
        v_send,
        v_recv,
        s_send,
        s_recv,
        x_send,
        x_recv,
        a_send,
        a_recv,
        b_send,
        b_recv,
        load_sem,
    ) = refs
    mx = lax.axis_index("gx")
    my = lax.axis_index("gy")

    def there(step_x, step_y):
        return (lax.rem(mx + step_x + nx, nx), lax.rem(my + step_y + ny, ny))

    barrier = pltpu.get_barrier_semaphore()
    peers_x = [(at, my) for at in others(mx, SPLIT_X)]
    peers_y = [(mx, at) for at in others(my, SPLIT_Y)]
    peers = peers_x + peers_y + [there(sx, sy) for sx, sy in WAYS[4:]]
    for peer in peers:
        pl.semaphore_signal(barrier, inc=1, device_id=peer, device_id_type=MESH)

    loads = [pltpu.make_async_copy(src, dst, load_sem.at[n]) for n, (src, dst) in enumerate(zip(given, here))]
    for n in LOAD_ORDER:
        loads[n].start()
    for n in LOAD_ORDER[:5]:
        loads[n].wait()

    lane = iota((ROWS, COLS), 1)
    group = lane // 32
    low = lane % 32 < 16
    own = [[vel[l, c].astype(F32) for c in range(2)] for l in range(LEVELS)]
    for c in range(2):
        packed = None
        for l in range(LEVELS):
            first = own[l][c] if l == 0 else shift_lanes(own[l][c], 32 * l)
            last = own[l][c] if l == 3 else shift_lanes(own[l][c], 32 * (l + 1))
            both = jnp.where(low, first, last)
            packed = both if l == 0 else jnp.where(group == l, both, packed)
        v_cols[pl.ds(16 * c, 16), :] = packed.astype(BF16)
        if c == 0:
            packed_first = packed
    for side in range(2):
        cut = slice(8, 16) if side == 0 else slice(0, 8)
        rows = jnp.concatenate([own[l][c][cut] for l in range(LEVELS) for c in range(2)], axis=0)
        v_rows[side] = rows.astype(BF16)
        v_corner[side] = jnp.concatenate([packed_first[cut], packed[cut]], axis=0).astype(BF16)
    st_own[0] = eta[...]
    st_own[1] = face[0]
    st_own[2] = face[1]
    st_own[3] = stor[...]
    st_own[4] = ocean[...].astype(F32)

    pl.semaphore_wait(barrier, len(peers))

    copies_v, copies_s = [], []
    for d in SEND_ORDER:
        sx, sy = WAYS[d]
        side = 0 if sy == 1 else 1
        if sy == 0:
            src, dst = v_cols, rv_cols.at[d]
        elif sx == 0:
            src, dst = v_rows.at[side], rv_rows.at[d - 2]
        else:
            src, dst = v_corner.at[side], rv_corner.at[d - 4]
        copy = pltpu.make_async_remote_copy(
            src_ref=src,
            dst_ref=dst,
            send_sem=v_send.at[d],
            recv_sem=v_recv.at[d],
            device_id=there(sx, sy),
            device_id_type=MESH,
        )
        copy.start()
        copies_v.append(copy)
    for d in SEND_ORDER:
        sx, sy = WAYS[d]
        if sy == 0:
            src, dst = st_own, rst_cols.at[d]
        else:
            src = st_own.at[:, pl.ds(8 if sy == 1 else 0, 8), :]
            dst = rst_rows.at[d - 2]
        copy = pltpu.make_async_remote_copy(
            src_ref=src,
            dst_ref=dst,
            send_sem=s_send.at[d],
            recv_sem=s_recv.at[d],
            device_id=there(sx, sy),
            device_id_type=MESH,
        )
        copy.start()
        copies_s.append(copy)

    for n in LOAD_ORDER[5:]:
        loads[n].wait()
    w1pad[...] = jnp.zeros_like(w1pad)
    for dy in range(5):
        for dx in range(5):
            taps = w1[dy, dx].astype(F32)
            for c in range(2):
                w1pad[dx, c, pl.ds(10 + dy, 1), pl.ds(0, 128)] = taps[c : c + 1]
                w1pad[dx, c, pl.ds(11 + dy, 1), pl.ds(128, 128)] = taps[c : c + 1]
    for s in range(6):
        for dx in range(5):
            for c in range(2):
                block = w1pad[dx, c, pl.ds(10 - 2 * s, 16), :]
                w1all[s, pl.ds(32 * dx + 16 * c, 16), :] = block.astype(BF16)
        w1all[s, pl.ds(160, 96), :] = jnp.zeros((96, 256), BF16)

    kept = [d1[pl.ds(m, 1), :].astype(F32).astype(BF16) for m in range(2)]
    nothing = jnp.zeros((64, 128), BF16)
    for dx in range(5):
        for dy in range(-1, 6):
            for m in range(2):
                block = w2[dy, dx] * kept[m] if 0 <= dy < 5 else nothing
                for b in range(2):
                    if 0 <= dy + b < 6:
                        o, a = divmod(dy + b, 2)
                        w2all[pl.ds(128 * b + 64 * m, 64), pl.ds(((o * 5 + dx) * 2 + a) * 128, 128)] = block

    w3f[...] = jnp.zeros_like(w3f)
    for ky in range(3):
        for dx in range(3):
            taps = w3[ky, dx].astype(F32) * 0.5
            for c in range(2):
                tap = taps[c : c + 1]
                both = jnp.concatenate([tap, tap], axis=1)
                for b in range(2):
                    w3f[pl.ds(8 * dx + 4 * c + b + 2 - ky, 1), pl.ds(128 * b, 128)] = both

    r = iota((M_V, 128), 0)
    lev = (r // 4) % 4
    x = 32 * (r % 4) + r // 16 - 5
    spot = jnp.where(x < 0, 512 + 32 * lev + 32 + x, jnp.where(x < 128, 128 * lev + x, 384 + 32 * lev + x))
    for k in range(5):
        pick[:, pl.ds(128 * k, 128)] = jnp.where(iota((M_V, 128), 1) + 128 * k == spot, 1.0, 0.0).astype(BF16)
    r = iota((512, 128), 0)
    spot = 128 * ((r // 4) % 4) + 32 * (r % 4) + r // 16
    for k in range(4):
        perm[:, pl.ds(128 * k, 128)] = jnp.where(iota((512, 128), 1) + 128 * k == spot, 1.0, 0.0).astype(BF16)

    has_south = jnp.where(my > 0, 1.0, 0.0)
    has_north = jnp.where(my < ny - 1, 1.0, 0.0)
    for copy in copies_v:
        copy.wait_recv()
    low8 = low[:8]
    south = rv_rows[0].astype(F32) * has_south
    north = rv_rows[1].astype(F32) * has_north
    from_w, from_e = rv_cols[0].astype(F32), rv_cols[1].astype(F32)
    from_sw, from_se = rv_corner[0].astype(F32), rv_corner[1].astype(F32)
    from_nw, from_ne = rv_corner[2].astype(F32), rv_corner[3].astype(F32)
    for c in range(2):
        for l in range(LEVELS):
            at = 8 * (2 * l + c)
            vx[l, c, pl.ds(0, 8), :] = south[at : at + 8]
            vx[l, c, pl.ds(8, 16), :] = own[l][c]
            vx[l, c, pl.ds(24, 8), :] = north[at : at + 8]
        cut = slice(8 * c, 8 * c + 8)
        vx[4, c, pl.ds(0, 8), :] = jnp.where(low8, from_se[cut], from_sw[cut]) * has_south
        cut16 = slice(16 * c, 16 * c + 16)
        vx[4, c, pl.ds(8, 16), :] = jnp.where(low, from_e[cut16], from_w[cut16])
        vx[4, c, pl.ds(24, 8), :] = jnp.where(low8, from_ne[cut], from_nw[cut]) * has_north
    for w in range(2):
        for k in range(5):
            for c in range(2):
                block = vx[k, c, pl.ds(3 + 10 * w, 16), :].astype(BF16)
                for rep in range(4):
                    bmat[pl.ds(128 * w + 32 * rep + 16 * c, 16), pl.ds(128 * k, 128)] = block
    umat[...] = dot_t(pick[...], bmat[...]).astype(BF16)

    bias1 = jnp.concatenate([b1[...].reshape(1, 128)] * 2, axis=1)
    upper = iota((1, 256), 1) // 128
    group1 = iota((M_1, 128), 1) // 32
    for w in range(2):
        lanes = pl.ds(128 * w, 128)
        near = umat[pl.ds(0, M_1), lanes]
        for g in range(1, 4):
            near = jnp.where(group1 == g, umat[pl.ds(16 * g, M_1), lanes], near)
        wide = jnp.concatenate([near, umat[pl.ds(64, M_1), lanes]], axis=1)

        def layer_one(j, carry, w=w, wide=wide):
            acc = dot(wide, w1all[j - 5 * w])
            row = my * ROWS + 2 * j - 3 + upper
            scale = jnp.where((row >= 0) & (row < ny * ROWS), KEEP_SCALE, 0.0)
            h1[j] = (jnp.maximum(acc + bias1, 0.0) * scale).astype(BF16)
            return carry

        lax.fori_loop(6 * w, 6 + 5 * w, layer_one, 0)

    bias2 = jnp.concatenate([b2[...].reshape(1, 64)] * 4, axis=1)
    keep2 = d2[...].astype(F32) * KEEP_SCALE
    keep2 = jnp.concatenate([keep2[0:1], keep2[1:2]] * 2, axis=1)
    zacc[...] = jnp.zeros_like(zacc)
    w3all = w3f[...].astype(BF16)

    def layer_two(first, spans):
        acc = None
        for o in range(3):
            for dx in range(5):
                lefts = [
                    h1[pl.ds(first + o, 3), pl.ds(16 * (dx + start), 16 * length), :].reshape(48 * length, 256)
                    for start, length in spans
                ]
                left = lefts[0] if len(lefts) == 1 else jnp.concatenate(lefts, axis=0)
                term = dot_t(left, w2all[:, pl.ds((o * 5 + dx) * 256, 256)])
                acc = term if acc is None else acc + term
        at = 0
        for start, length in spans:
            for q in range(3):
                row = my * ROWS + 2 * (first + q) - 1 + upper
                scale = jnp.where((row >= 0) & (row < ny * ROWS), keep2, 0.0)
                hidden = jnp.maximum(acc[at : at + 16 * length] + bias2, 0.0) * scale
                h2[first + q, pl.ds(16 * start, 16 * length), :] = hidden.astype(BF16)
                at += 16 * length

    def layer_three(target, first):
        for q in range(3):
            z = dot_t(w3all, h2[first + q])
            part = z[0:8, 0:512] + z[8:16, 16:528] + z[16:24, 32:544]
            for c in range(2):
                for t in range(4):
                    at = pl.ds(2 * (first + q) + t, 1)
                    zacc[target, c, at, :] = zacc[target, c, at, :] + part[4 * c + t : 4 * c + t + 1]

    def finish(mixed, fx, f):
        high = mixed.astype(BF16)
        rest = (mixed - high.astype(F32)).astype(BF16)
        out = dot(jnp.concatenate([high, rest], axis=0), perm[...])
        out = out[0:32] + out[32:64]
        for c in range(2):
            total = None
            for l in range(LEVELS):
                forcing = out[16 * c : 16 * c + 16, 128 * l : 128 * l + 128] + b3[c]
                if f is not None:
                    f[l, c] = forcing
                term = thick[l] * (vel[l, c].astype(F32) + forcing)
                total = term if total is None else total + term
            fx[c] = total

    def outer_rows(n, carry):
        layer_two(6 * n, [(0, XO_2)])
        return carry

    lax.fori_loop(0, 2, outer_rows, 0)
    h2[pl.ds(3, 3), pl.ds(16 * EDGE_W, 16 * (EDGE_E - EDGE_W)), :] = jnp.zeros((3, 16 * (EDGE_E - EDGE_W), 256), BF16)
    layer_two(3, [(0, EDGE_W), (EDGE_E, XO_2 - EDGE_E)])
    layer_three(0, 0)
    layer_three(0, 6)
    layer_three(1, 3)
    sums01 = [zacc[0, c, pl.ds(2, 16), :] + zacc[1, c, pl.ds(2, 16), :] for c in range(2)]
    finish(jnp.concatenate(sums01, axis=0), fx_own, None)

    copies_x = []
    for d in SEND_ORDER:
        sx, sy = WAYS[d]
        if sy == 0:
            src, dst = fx_own, rfx_cols.at[d]
        else:
            src = fx_own.at[:, pl.ds(8 if sy == 1 else 0, 8), :]
            dst = rfx_rows.at[d - 2]
        copy = pltpu.make_async_remote_copy(
            src_ref=src,
            dst_ref=dst,
            send_sem=x_send.at[d],
            recv_sem=x_recv.at[d],
            device_id=there(sx, sy),
            device_id_type=MESH,
        )
        copy.start()
        copies_x.append(copy)

    layer_two(3, [(EDGE_W, EDGE_E - EDGE_W)])
    layer_three(2, 3)
    sums02 = [zacc[0, c, pl.ds(2, 16), :] + zacc[2, c, pl.ds(2, 16), :] for c in range(2)]
    finish(jnp.concatenate(sums02, axis=0), fx_all, f_out)

    for copy in copies_s:
        copy.wait_recv()

    side = iota((ROWS, COLS), 1) < 64
    side8 = side[:8]

    def widened(own_ref, cols_ref, rows_ref, k):
        middle = jnp.concatenate([own_ref[k], jnp.where(side, cols_ref[1, k], cols_ref[0, k])], axis=1)
        below = jnp.concatenate([rows_ref[0, k], jnp.where(side8, rows_ref[3, k], rows_ref[2, k])], axis=1)
        above = jnp.concatenate([rows_ref[1, k], jnp.where(side8, rows_ref[5, k], rows_ref[4, k])], axis=1)
        return jnp.concatenate([below, middle, above], axis=0)

    eta_w, east_w, north_w, stor_w, sea = [widened(st_own, rst_cols, rst_rows, k) for k in range(5)]
    place = iota(sea.shape, 0) - 8 + my * ROWS
    sea = jnp.where((place >= 0) & (place < ny * ROWS), sea, 0.0)
    open_east = sea * shift_lanes(sea, -1)
    open_north = sea * shift_rows(sea, -1)
    coef_east = east_w * open_east
    coef_north = north_w * open_north
    coef_west = shift_lanes(coef_east, 1)
    coef_south = shift_rows(coef_north, 1)
    diagonal = stor_w + coef_east + coef_west + coef_north + coef_south

    def operate(field):
        return (
            diagonal * field
            - coef_east * shift_lanes(field, -1)
            - coef_west * shift_lanes(field, 1)
            - coef_north * shift_rows(field, -1)
            - coef_south * shift_rows(field, 1)
        )

    known = stor_w * eta_w - operate(eta_w)
    for copy in copies_x:
        copy.wait_recv()
    zonal, merid = [widened(fx_all, rfx_cols, rfx_rows, k) for k in range(2)]
    flux_east = zonal * open_east
    flux_north = merid * open_north
    diverge = flux_east - shift_lanes(flux_east, 1) + flux_north - shift_rows(flux_north, 1)
    k0 = known - diverge
    k1 = operate(k0)
    k2 = operate(k1)
    k3 = operate(k2)
    k0, k1, k2, k3 = [k[8:24, 0:128] for k in (k0, k1, k2, k3)]

    lane1 = iota((1, 128), 1)
    sums = jnp.zeros((1, 128), F32)
    for n, (a, b) in enumerate(((k0, k0), (k0, k1), (k1, k1), (k1, k2), (k2, k2), (k2, k3))):
        total = jnp.sum(jnp.sum(a * b, axis=0, keepdims=True), axis=1, keepdims=True)
        sums = jnp.where(lane1 == n, total, sums)

    def exchange(values, mine, got, send, recv, targets):
        mine[...] = values
        copies = []
        for k, target in enumerate(targets):
            copy = pltpu.make_async_remote_copy(
                src_ref=mine,
                dst_ref=got.at[k],
                send_sem=send.at[k],
                recv_sem=recv.at[k],
                device_id=target,
                device_id_type=MESH,
            )
            copy.start()
            copies.append(copy)
        for copy in copies:
            copy.wait_recv()
        return values + jnp.sum(got[...], axis=0), copies

    sums, copies_a = exchange(sums, red_a, got_a, a_send, a_recv, peers_x)
    sums, copies_b = exchange(sums, red_b, got_b, b_send, b_recv, peers_y)
    m0, m1, m2, m3, m4, m5 = [
        jnp.sum(jnp.where(lane1 == n, sums, 0.0), axis=1, keepdims=True) for n in range(6)
    ]

    def over(value, scale):
        fine = value > 1e-6 * scale
        return jnp.where(fine, 1.0 / jnp.where(fine, value, 1.0), 0.0)

    inv0 = over(m1, jnp.zeros_like(m1))
    l1 = m2 * inv0
    l2 = m3 * inv0
    p1 = m3 - l1 * m2
    inv1 = over(p1, m3)
    e21 = m4 - l2 * m2
    l21 = e21 * inv1
    p2 = m5 - l2 * m3 - l21 * e21
    inv2 = jnp.where(inv1 > 0.0, over(p2, m5), 0.0)
    z1 = m1 - l1 * m0
    z2 = m2 - l2 * m0 - l21 * z1
    c2 = z2 * inv2
    c1 = z1 * inv1 - l21 * c2
    c0 = m0 * inv0 - l1 * c1 - l2 * c2
    e_out[...] = eta[...] + c0 * k0 + c1 * k1 + c2 * k2

    for copy in copies_v + copies_s + copies_x + copies_a + copies_b:
        copy.wait_send()


def body(nx, ny, *args):
    vmem = pl.BlockSpec(memory_space=pltpu.VMEM)
    args = list(args)
    args[1] = jnp.transpose(args[1], (1, 2, 0, 3))
    args[5] = jnp.transpose(args[5], (1, 2, 0, 3))
    here = [(pltpu.SMEM if n in (6, 9) else pltpu.VMEM)(a.shape, a.dtype) for n, a in enumerate(args)]
    dma = pltpu.SemaphoreType.DMA
    V = pltpu.VMEM
    return pl.pallas_call(
        functools.partial(kernel, nx, ny),
        out_shape=(
            jax.ShapeDtypeStruct((LEVELS, 2, ROWS, COLS), F32),
            jax.ShapeDtypeStruct((ROWS, COLS), F32),
        ),
        in_specs=[pl.BlockSpec(memory_space=pltpu.HBM)] * 14,
        out_specs=(vmem, vmem),
        scratch_shapes=here + [
            V((2, 64, 128), BF16),
            V((32, 128), BF16),
            V((2, 16, 128), BF16),
            V((5, ROWS, COLS), F32),
            V((2, ROWS, COLS), F32),
            V((2, ROWS, COLS), F32),
            V((2, 64, 128), BF16),
            V((2, 32, 128), BF16),
            V((4, 16, 128), BF16),
            V((2, 5, ROWS, COLS), F32),
            V((6, 5, 8, COLS), F32),
            V((2, 2, ROWS, COLS), F32),
            V((6, 2, 8, COLS), F32),
            V((1, 128), F32),
            V((1, 128), F32),
            V((nx - 1, 1, 128), F32),
            V((ny - 1, 1, 128), F32),
            V((5, 2, 32, 128), F32),
            V((256, 640), BF16),
            V((M_V, 640), BF16),
            V((M_V, 256), BF16),
            V((5, 2, 32, 256), F32),
            V((6, 256, 256), BF16),
            V((256, 3840), BF16),
            V((32, 256), F32),
            V((11, M_1, 256), BF16),
            V((9, M_2, 256), BF16),
            V((3, 2, 24, 512), F32),
            V((512, 512), BF16),
            dma((8,)),
            dma((8,)),
            dma((8,)),
            dma((8,)),
            dma((8,)),
            dma((8,)),
            dma((nx - 1,)),
            dma((nx - 1,)),
            dma((ny - 1,)),
            dma((ny - 1,)),
            dma((14,)),
        ],
        compiler_params=pltpu.CompilerParams(
            collective_id=0, has_side_effects=True, vmem_limit_bytes=60 * 2**20
        ),
        name="ocean_step",
    )(*args)


def solution(mesh):
    nx, ny = mesh.shape["gx"], mesh.shape["gy"]
    tile = P("gy", "gx")
    stacked = P(None, "gy", "gx")
    levels = P(None, None, "gy", "gx")
    in_specs = (levels,) + (P(),) * 9 + (tile, stacked, tile, tile)
    return jax.shard_map(
        functools.partial(body, nx, ny),
        mesh=mesh,
        in_specs=in_specs,
        out_specs=(levels, tile),
        check_vma=False,
    )
```

```python
import functools
import itertools

import jax
import jax.numpy as jnp
from jax import lax
from jax.experimental import pallas as pl
from jax.experimental.pallas import tpu as pltpu
from jax.sharding import PartitionSpec as P

MESH = pl.DeviceIdType.MESH
F32 = jnp.float32
BF16 = jnp.bfloat16
KEEP_SCALE = 4.0 / 3.0

WAYS = ((1, 0), (-1, 0), (0, 1), (0, -1), (1, 1), (-1, 1), (1, -1), (-1, -1))

ROWS, COLS, LEVELS = 16, 128, 4
SEND_ORDER = (4, 5, 6, 7, 2, 3, 0, 1)

SPLIT_X = ((2, 2), (4, 1), (2, 0))
SPLIT_Y = ((2, 1), (8, 1))

LOAD_ORDER = (0, 10, 11, 12, 13, 1, 7, 3, 5, 2, 4, 6, 8, 9)

XO_V, XO_1, XO_2 = 42, 38, 34
EDGE_W, EDGE_E = 5, 28
M_V, M_1, M_2 = 16 * XO_V, 16 * XO_1, 16 * XO_2


def iota(shape, dim):
    return lax.broadcasted_iota(jnp.int32, shape, dim)


def dot_t(a, b):
    return lax.dot_general(a, b, (((1,), (1,)), ((), ())), preferred_element_type=F32)


def dot(a, b):
    return jnp.dot(a, b, preferred_element_type=F32)


def others(index, split):
    sizes = [size for size, _ in split]
    steps = list(itertools.product(*[range(size) for size in sizes]))[1:]
    steps.sort(key=lambda step: -sum(hops * min(k, size - k) for k, (size, hops) in zip(step, split)))
    found = []
    for step in steps:
        at, stride = 0, 1
        for k, size in reversed(list(zip(step, sizes))):
            digit = lax.rem(lax.div(index, jnp.int32(stride)), jnp.int32(size))
            at = at + lax.rem(digit + k, jnp.int32(size)) * stride
            stride *= size
        found.append(at)
    return found


def shift_lanes(x, by):
    return pltpu.roll(x, by % x.shape[1], 1)


def shift_rows(x, by):
    return pltpu.roll(x, by % x.shape[0], 0)


def kernel(
    nx,
    ny,
    *refs,
):
    given, refs = refs[:14], refs[14:]
    (f_out, e_out), refs = refs[:2], refs[2:]
    here, refs = refs[:14], refs[14:]
    vel, w1, b1, w2, b2, w3, b3, d1, d2, thick, eta, face, stor, ocean = here
    (
        v_rows,
        v_cols,
        v_corner,
        st_own,
        fx_own,
        fx_all,
        rv_rows,
        rv_cols,
        rv_corner,
        rst_cols,
        rst_rows,
        rfx_cols,
        rfx_rows,
        red_a,
        red_b,
        got_a,
        got_b,
        vx,
        bmat,
        pick,
        umat,
        w1pad,
        w1all,
        w2all,
        w3f,
        h1,
        h2,
        zacc,
        mixed_out,
        perm,
        v_send,
        v_recv,
        s_send,
        s_recv,
        x_send,
        x_recv,
        a_send,
        a_recv,
        b_send,
        b_recv,
        load_sem,
    ) = refs
    mx = lax.axis_index("gx")
    my = lax.axis_index("gy")

    def there(step_x, step_y):
        return (lax.rem(mx + step_x + nx, nx), lax.rem(my + step_y + ny, ny))

    barrier = pltpu.get_barrier_semaphore()
    peers_x = [(at, my) for at in others(mx, SPLIT_X)]
    peers_y = [(mx, at) for at in others(my, SPLIT_Y)]
    peers = [there(sx, sy) for sx, sy in WAYS[4:]] + peers_x[::-1] + peers_y[::-1]
    loads = [pltpu.make_async_copy(src, dst, load_sem.at[n]) for n, (src, dst) in enumerate(zip(given, here))]
    loads[0].start()
    for peer in peers:
        pl.semaphore_signal(barrier, inc=1, device_id=peer, device_id_type=MESH)
    for n in LOAD_ORDER[1:]:
        loads[n].start()
    loads[0].wait()

    lane = iota((ROWS, COLS), 1)
    group = lane // 32
    low = lane % 32 < 16
    own = [[vel[l, c].astype(F32) for c in range(2)] for l in range(LEVELS)]
    for c in range(2):
        packed = None
        for l in range(LEVELS):
            first = own[l][c] if l == 0 else shift_lanes(own[l][c], 32 * l)
            last = own[l][c] if l == 3 else shift_lanes(own[l][c], 32 * (l + 1))
            both = jnp.where(low, first, last)
            packed = both if l == 0 else jnp.where(group == l, both, packed)
        v_cols[pl.ds(16 * c, 16), :] = packed.astype(BF16)
        if c == 0:
            packed_first = packed
    for side in range(2):
        cut = slice(8, 16) if side == 0 else slice(0, 8)
        rows = jnp.concatenate([own[l][c][cut] for l in range(LEVELS) for c in range(2)], axis=0)
        v_rows[side] = rows.astype(BF16)
        v_corner[side] = jnp.concatenate([packed_first[cut], packed[cut]], axis=0).astype(BF16)

    pl.semaphore_wait(barrier, len(peers))

    copies_v, copies_s = [], []
    for d in SEND_ORDER:
        sx, sy = WAYS[d]
        side = 0 if sy == 1 else 1
        if sy == 0:
            src, dst = v_cols, rv_cols.at[d]
        elif sx == 0:
            src, dst = v_rows.at[side], rv_rows.at[d - 2]
        else:
            src, dst = v_corner.at[side], rv_corner.at[d - 4]
        copy = pltpu.make_async_remote_copy(
            src_ref=src,
            dst_ref=dst,
            send_sem=v_send.at[d],
            recv_sem=v_recv.at[d],
            device_id=there(sx, sy),
            device_id_type=MESH,
        )
        copy.start()
        copies_v.append(copy)
    for n in LOAD_ORDER[1:5]:
        loads[n].wait()
    st_own[0] = eta[...]
    st_own[1] = face[0]
    st_own[2] = face[1]
    st_own[3] = stor[...]
    st_own[4] = ocean[...].astype(F32)
    for d in SEND_ORDER:
        sx, sy = WAYS[d]
        if sy == 0:
            src, dst = st_own, rst_cols.at[d]
        else:
            src = st_own.at[:, pl.ds(8 if sy == 1 else 0, 8), :]
            dst = rst_rows.at[d - 2]
        copy = pltpu.make_async_remote_copy(
            src_ref=src,
            dst_ref=dst,
            send_sem=s_send.at[d],
            recv_sem=s_recv.at[d],
            device_id=there(sx, sy),
            device_id_type=MESH,
        )
        copy.start()
        copies_s.append(copy)

    for n in LOAD_ORDER[5:]:
        loads[n].wait()
    w1pad[...] = jnp.zeros_like(w1pad)
    for dy in range(5):
        for dx in range(5):
            taps = w1[dy, dx].astype(F32)
            for c in range(2):
                w1pad[dx, c, pl.ds(10 + dy, 1), pl.ds(0, 128)] = taps[c : c + 1]
                w1pad[dx, c, pl.ds(11 + dy, 1), pl.ds(128, 128)] = taps[c : c + 1]
    for s in range(6):
        for dx in range(5):
            for c in range(2):
                block = w1pad[dx, c, pl.ds(10 - 2 * s, 16), :]
                w1all[s, pl.ds(32 * dx + 16 * c, 16), :] = block.astype(BF16)
        w1all[s, pl.ds(160, 96), :] = jnp.zeros((96, 256), BF16)

    kept = [d1[pl.ds(m, 1), :].astype(F32).astype(BF16) for m in range(2)]
    nothing = jnp.zeros((64, 128), BF16)
    for dx in range(5):
        for dy in range(-1, 6):
            for m in range(2):
                block = w2[dy, dx] * kept[m] if 0 <= dy < 5 else nothing
                for b in range(2):
                    if 0 <= dy + b < 6:
                        o, a = divmod(dy + b, 2)
                        w2all[pl.ds(128 * b + 64 * m, 64), pl.ds(((o * 5 + dx) * 2 + a) * 128, 128)] = block

    w3f[...] = jnp.zeros_like(w3f)
    for ky in range(3):
        for dx in range(3):
            taps = w3[ky, dx].astype(F32) * 0.5
            for c in range(2):
                tap = taps[c : c + 1]
                both = jnp.concatenate([tap, tap], axis=1)
                for b in range(2):
                    w3f[pl.ds(8 * dx + 2 * (b + 2 - ky) + c, 1), pl.ds(128 * b, 128)] = both

    r = iota((M_V, 128), 0)
    lev = (r // 4) % 4
    x = 32 * (r % 4) + r // 16 - 5
    spot = jnp.where(x < 0, 512 + 32 * lev + 32 + x, jnp.where(x < 128, 128 * lev + x, 384 + 32 * lev + x))
    for k in range(5):
        pick[:, pl.ds(128 * k, 128)] = jnp.where(iota((M_V, 128), 1) + 128 * k == spot, 1.0, 0.0).astype(BF16)
    r = iota((512, 128), 0)
    spot = 128 * ((r // 4) % 4) + 32 * (r % 4) + r // 16
    for k in range(4):
        perm[:, pl.ds(128 * k, 128)] = jnp.where(iota((512, 128), 1) + 128 * k == spot, 1.0, 0.0).astype(BF16)

    has_south = jnp.where(my > 0, 1.0, 0.0)
    has_north = jnp.where(my < ny - 1, 1.0, 0.0)
    for copy in copies_v:
        copy.wait_recv()
    low8 = low[:8]
    south = rv_rows[0].astype(F32) * has_south
    north = rv_rows[1].astype(F32) * has_north
    from_w, from_e = rv_cols[0].astype(F32), rv_cols[1].astype(F32)
    from_sw, from_se = rv_corner[0].astype(F32), rv_corner[1].astype(F32)
    from_nw, from_ne = rv_corner[2].astype(F32), rv_corner[3].astype(F32)
    for c in range(2):
        for l in range(LEVELS):
            at = 8 * (2 * l + c)
            vx[l, c, pl.ds(0, 8), :] = south[at : at + 8]
            vx[l, c, pl.ds(8, 16), :] = own[l][c]
            vx[l, c, pl.ds(24, 8), :] = north[at : at + 8]
        cut = slice(8 * c, 8 * c + 8)
        vx[4, c, pl.ds(0, 8), :] = jnp.where(low8, from_se[cut], from_sw[cut]) * has_south
        cut16 = slice(16 * c, 16 * c + 16)
        vx[4, c, pl.ds(8, 16), :] = jnp.where(low, from_e[cut16], from_w[cut16])
        vx[4, c, pl.ds(24, 8), :] = jnp.where(low8, from_ne[cut], from_nw[cut]) * has_north
    for w in range(2):
        for k in range(5):
            for c in range(2):
                block = vx[k, c, pl.ds(3 + 10 * w, 16), :].astype(BF16)
                for rep in range(4):
                    bmat[pl.ds(128 * w + 32 * rep + 16 * c, 16), pl.ds(128 * k, 128)] = block
    umat[...] = dot_t(pick[...], bmat[...]).astype(BF16)

    bias1 = jnp.concatenate([b1[...].reshape(1, 128)] * 2, axis=1)
    upper = iota((1, 256), 1) // 128
    group1 = iota((M_1, 128), 1) // 32
    for w in range(2):
        lanes = pl.ds(128 * w, 128)
        near = umat[pl.ds(0, M_1), lanes]
        for g in range(1, 4):
            near = jnp.where(group1 == g, umat[pl.ds(16 * g, M_1), lanes], near)
        wide = jnp.concatenate([near, umat[pl.ds(64, M_1), lanes]], axis=1)

        for j in range(6 * w, 6 + 5 * w):
            acc = dot(wide, w1all[j - 5 * w])
            row = my * ROWS + 2 * j - 3 + upper
            scale = jnp.where((row >= 0) & (row < ny * ROWS), KEEP_SCALE, 0.0)
            h1[j] = (jnp.maximum(acc + bias1, 0.0) * scale).astype(BF16)

    bias2 = jnp.concatenate([b2[...].reshape(1, 64)] * 4, axis=1)
    keep2 = d2[...].astype(F32) * KEEP_SCALE
    keep2 = jnp.concatenate([keep2[0:1], keep2[1:2]] * 2, axis=1)
    w3all = w3f[...].astype(BF16)

    def layer_two(first, spans):
        acc = None
        for o in range(3):
            for dx in range(5):
                lefts = [
                    h1[pl.ds(first + o, 3), pl.ds(16 * (dx + start), 16 * length), :].reshape(48 * length, 256)
                    for start, length in spans
                ]
                left = lefts[0] if len(lefts) == 1 else jnp.concatenate(lefts, axis=0)
                term = dot_t(left, w2all[:, pl.ds((o * 5 + dx) * 256, 256)])
                acc = term if acc is None else acc + term
        at = 0
        for start, length in spans:
            for q in range(3):
                row = my * ROWS + 2 * (first + q) - 1 + upper
                scale = jnp.where((row >= 0) & (row < ny * ROWS), keep2, 0.0)
                hidden = jnp.maximum(acc[at : at + 16 * length] + bias2, 0.0) * scale
                h2[first + q, pl.ds(16 * start, 16 * length), :] = hidden.astype(BF16)
                at += 16 * length

    def layer_three(first):
        for i in range(first, first + 3):
            z = dot_t(w3all, h2[i])
            zacc[i] = z[0:8, 0:512] + z[8:16, 16:528] + z[16:24, 32:544]

    def finish(fx, f):
        mixed = jnp.concatenate([zacc[p, pl.ds(4, 4), :] + zacc[p + 1, pl.ds(0, 4), :] for p in range(8)], axis=0)
        high = mixed.astype(BF16)
        rest = (mixed - high.astype(F32)).astype(BF16)
        out = dot(jnp.concatenate([high, rest], axis=0), perm[...])
        for l in range(LEVELS):
            lanes = slice(128 * l, 128 * l + 128)
            mixed_out[l] = out[0:32, lanes] + out[32:64, lanes]
        for c in range(2):
            total = None
            for l in range(LEVELS):
                forcing = mixed_out[l, pl.ds(c, 16, stride=2), :] + b3[c]
                if f is not None:
                    f[l, c] = forcing
                term = thick[l] * (vel[l, c].astype(F32) + forcing)
                total = term if total is None else total + term
            fx[c] = total

    def outer_rows(n, carry):
        layer_two(6 * n, [(0, XO_2)])
        return carry

    lax.fori_loop(0, 2, outer_rows, 0)
    h2[pl.ds(3, 3), pl.ds(16 * EDGE_W, 16 * (EDGE_E - EDGE_W)), :] = jnp.zeros((3, 16 * (EDGE_E - EDGE_W), 256), BF16)
    layer_two(3, [(0, EDGE_W), (EDGE_E, XO_2 - EDGE_E)])
    layer_three(0)
    layer_three(6)
    layer_three(3)
    finish(fx_own, None)

    copies_x = []
    for d in SEND_ORDER:
        sx, sy = WAYS[d]
        if sy == 0:
            src, dst = fx_own, rfx_cols.at[d]
        else:
            src = fx_own.at[:, pl.ds(8 if sy == 1 else 0, 8), :]
            dst = rfx_rows.at[d - 2]
        copy = pltpu.make_async_remote_copy(
            src_ref=src,
            dst_ref=dst,
            send_sem=x_send.at[d],
            recv_sem=x_recv.at[d],
            device_id=there(sx, sy),
            device_id_type=MESH,
        )
        copy.start()
        copies_x.append(copy)

    layer_two(3, [(EDGE_W, EDGE_E - EDGE_W)])
    layer_three(3)
    finish(fx_all, f_out)

    for copy in copies_s:
        copy.wait_recv()

    side = iota((ROWS, COLS), 1) < 64
    side8 = side[:8]

    def widened(own_ref, cols_ref, rows_ref, k):
        middle = jnp.concatenate([own_ref[k], jnp.where(side, cols_ref[1, k], cols_ref[0, k])], axis=1)
        below = jnp.concatenate([rows_ref[0, k], jnp.where(side8, rows_ref[3, k], rows_ref[2, k])], axis=1)
        above = jnp.concatenate([rows_ref[1, k], jnp.where(side8, rows_ref[5, k], rows_ref[4, k])], axis=1)
        return jnp.concatenate([below, middle, above], axis=0)

    eta_w, east_w, north_w, stor_w, sea = [widened(st_own, rst_cols, rst_rows, k) for k in range(5)]
    place = iota(sea.shape, 0) - 8 + my * ROWS
    sea = jnp.where((place >= 0) & (place < ny * ROWS), sea, 0.0)
    open_east = sea * shift_lanes(sea, -1)
    open_north = sea * shift_rows(sea, -1)
    coef_east = east_w * open_east
    coef_north = north_w * open_north
    coef_west = shift_lanes(coef_east, 1)
    coef_south = shift_rows(coef_north, 1)
    diagonal = stor_w + coef_east + coef_west + coef_north + coef_south

    def operate(field):
        return (
            diagonal * field
            - coef_east * shift_lanes(field, -1)
            - coef_west * shift_lanes(field, 1)
            - coef_north * shift_rows(field, -1)
            - coef_south * shift_rows(field, 1)
        )

    known = stor_w * eta_w - operate(eta_w)
    for copy in copies_x:
        copy.wait_recv()
    zonal, merid = [widened(fx_all, rfx_cols, rfx_rows, k) for k in range(2)]
    flux_east = zonal * open_east
    flux_north = merid * open_north
    diverge = flux_east - shift_lanes(flux_east, 1) + flux_north - shift_rows(flux_north, 1)
    k0 = known - diverge
    k1 = operate(k0)
    k2 = operate(k1)
    k3 = operate(k2)
    k0, k1, k2, k3 = [k[8:24, 0:128] for k in (k0, k1, k2, k3)]

    lane1 = iota((1, 128), 1)
    sums = jnp.zeros((1, 128), F32)
    for n, (a, b) in enumerate(((k0, k0), (k0, k1), (k1, k1), (k1, k2), (k2, k2), (k2, k3))):
        total = jnp.sum(jnp.sum(a * b, axis=0, keepdims=True), axis=1, keepdims=True)
        sums = jnp.where(lane1 == n, total, sums)

    def exchange(values, mine, got, send, recv, targets):
        mine[...] = values
        copies = []
        for k, target in enumerate(targets):
            copy = pltpu.make_async_remote_copy(
                src_ref=mine,
                dst_ref=got.at[k],
                send_sem=send.at[k],
                recv_sem=recv.at[k],
                device_id=target,
                device_id_type=MESH,
            )
            copy.start()
            copies.append(copy)
        for copy in copies:
            copy.wait_recv()
        return values + jnp.sum(got[...], axis=0), copies

    sums, copies_a = exchange(sums, red_a, got_a, a_send, a_recv, peers_x)
    sums, copies_b = exchange(sums, red_b, got_b, b_send, b_recv, peers_y)
    m0, m1, m2, m3, m4, m5 = [
        jnp.sum(jnp.where(lane1 == n, sums, 0.0), axis=1, keepdims=True) for n in range(6)
    ]

    def over(value, scale):
        fine = value > 1e-6 * scale
        return jnp.where(fine, 1.0 / jnp.where(fine, value, 1.0), 0.0)

    inv0 = over(m1, jnp.zeros_like(m1))
    l1 = m2 * inv0
    l2 = m3 * inv0
    p1 = m3 - l1 * m2
    inv1 = over(p1, m3)
    e21 = m4 - l2 * m2
    l21 = e21 * inv1
    p2 = m5 - l2 * m3 - l21 * e21
    inv2 = jnp.where(inv1 > 0.0, over(p2, m5), 0.0)
    z1 = m1 - l1 * m0
    z2 = m2 - l2 * m0 - l21 * z1
    c2 = z2 * inv2
    c1 = z1 * inv1 - l21 * c2
    c0 = m0 * inv0 - l1 * c1 - l2 * c2
    e_out[...] = eta[...] + c0 * k0 + c1 * k1 + c2 * k2

    for copy in copies_v + copies_s + copies_x + copies_a + copies_b:
        copy.wait_send()


def body(nx, ny, *args):
    vmem = pl.BlockSpec(memory_space=pltpu.VMEM)
    args = list(args)
    args[1] = jnp.transpose(args[1], (1, 2, 0, 3))
    args[5] = jnp.transpose(args[5], (1, 2, 0, 3))
    here = [(pltpu.SMEM if n in (6, 9) else pltpu.VMEM)(a.shape, a.dtype) for n, a in enumerate(args)]
    dma = pltpu.SemaphoreType.DMA
    V = pltpu.VMEM
    return pl.pallas_call(
        functools.partial(kernel, nx, ny),
        out_shape=(
            pltpu.VMEM((LEVELS, 2, ROWS, COLS), F32),
            pltpu.VMEM((ROWS, COLS), F32),
        ),
        in_specs=[pl.BlockSpec(memory_space=pltpu.HBM)] * 14,
        out_specs=(vmem, vmem),
        scratch_shapes=here + [
            V((2, 64, 128), BF16),
            V((32, 128), BF16),
            V((2, 16, 128), BF16),
            V((5, ROWS, COLS), F32),
            V((2, ROWS, COLS), F32),
            V((2, ROWS, COLS), F32),
            V((2, 64, 128), BF16),
            V((2, 32, 128), BF16),
            V((4, 16, 128), BF16),
            V((2, 5, ROWS, COLS), F32),
            V((6, 5, 8, COLS), F32),
            V((2, 2, ROWS, COLS), F32),
            V((6, 2, 8, COLS), F32),
            V((1, 128), F32),
            V((1, 128), F32),
            V((nx - 1, 1, 128), F32),
            V((ny - 1, 1, 128), F32),
            V((5, 2, 32, 128), F32),
            V((256, 640), BF16),
            V((M_V, 640), BF16),
            V((M_V, 256), BF16),
            V((5, 2, 32, 256), F32),
            V((6, 256, 256), BF16),
            V((256, 3840), BF16),
            V((32, 256), F32),
            V((11, M_1, 256), BF16),
            V((9, M_2, 256), BF16),
            V((9, 8, 512), F32),
            V((LEVELS, 32, 128), F32),
            V((512, 512), BF16),
            dma((8,)),
            dma((8,)),
            dma((8,)),
            dma((8,)),
            dma((8,)),
            dma((8,)),
            dma((nx - 1,)),
            dma((nx - 1,)),
            dma((ny - 1,)),
            dma((ny - 1,)),
            dma((14,)),
        ],
        compiler_params=pltpu.CompilerParams(
            collective_id=0, has_side_effects=True, vmem_limit_bytes=60 * 2**20
        ),
        name="ocean_step",
    )(*args)


def solution(mesh):
    nx, ny = mesh.shape["gx"], mesh.shape["gy"]
    tile = P("gy", "gx")
    stacked = P(None, "gy", "gx")
    levels = P(None, None, "gy", "gx")
    in_specs = (levels,) + (P(),) * 9 + (tile, stacked, tile, tile)
    return jax.shard_map(
        functools.partial(body, nx, ny),
        mesh=mesh,
        in_specs=in_specs,
        out_specs=(levels, tile),
        check_vma=False,
    )
```

```python
import functools
import itertools

import jax
import jax.numpy as jnp
from jax import lax
from jax.experimental import pallas as pl
from jax.experimental.pallas import tpu as pltpu
from jax.sharding import PartitionSpec as P

MESH = pl.DeviceIdType.MESH
F32 = jnp.float32
BF16 = jnp.bfloat16
KEEP_SCALE = 4.0 / 3.0

WAYS = ((1, 0), (-1, 0), (0, 1), (0, -1), (1, 1), (-1, 1), (1, -1), (-1, -1))

ROWS, COLS, LEVELS = 16, 128, 4
SEND_ORDER = (4, 5, 6, 7, 2, 3, 0, 1)

SPLIT_X = ((2, 2), (4, 1), (2, 0))
SPLIT_Y = ((2, 1), (8, 1))

LOAD_ORDER = (0, 10, 11, 12, 13, 1, 7, 3, 5, 2, 4, 6, 8, 9)

XO_V, XO_1, XO_2 = 42, 38, 34
U_2 = XO_2 // 2
EDGE_W, EDGE_E = 3, 14
M_V, M_1, M_2 = 16 * XO_V, 16 * XO_1, 16 * XO_2


def iota(shape, dim):
    return lax.broadcasted_iota(jnp.int32, shape, dim)


def dot_t(a, b):
    return lax.dot_general(a, b, (((1,), (1,)), ((), ())), preferred_element_type=F32)


def dot(a, b):
    return jnp.dot(a, b, preferred_element_type=F32)


def others(index, split):
    sizes = [size for size, _ in split]
    steps = list(itertools.product(*[range(size) for size in sizes]))[1:]
    steps.sort(key=lambda step: -sum(hops * min(k, size - k) for k, (size, hops) in zip(step, split)))
    found = []
    for step in steps:
        at, stride = 0, 1
        for k, size in reversed(list(zip(step, sizes))):
            digit = lax.rem(lax.div(index, jnp.int32(stride)), jnp.int32(size))
            at = at + lax.rem(digit + k, jnp.int32(size)) * stride
            stride *= size
        found.append(at)
    return found


def shift_lanes(x, by):
    return pltpu.roll(x, by % x.shape[1], 1)


def shift_rows(x, by):
    return pltpu.roll(x, by % x.shape[0], 0)


def kernel(
    nx,
    ny,
    *refs,
):
    given, refs = refs[:14], refs[14:]
    (f_out, e_out), refs = refs[:2], refs[2:]
    here, refs = refs[:14], refs[14:]
    vel, w1, b1, w2, b2, w3, b3, d1, d2, thick, eta, face, stor, ocean = here
    (
        v_rows,
        v_cols,
        v_corner,
        st_own,
        fx_own,
        fx_all,
        rv_rows,
        rv_cols,
        rv_corner,
        rst_cols,
        rst_rows,
        rfx_cols,
        rfx_rows,
        red_a,
        red_b,
        got_a,
        got_b,
        vx,
        bmat,
        pick,
        umat,
        w1pad,
        w1all,
        w2all,
        w3f,
        h1,
        mixed1,
        h2,
        zacc,
        mixed_out,
        perm,
        v_send,
        v_recv,
        s_send,
        s_recv,
        x_send,
        x_recv,
        a_send,
        a_recv,
        b_send,
        b_recv,
        load_sem,
    ) = refs
    mx = lax.axis_index("gx")
    my = lax.axis_index("gy")

    def there(step_x, step_y):
        return (lax.rem(mx + step_x + nx, nx), lax.rem(my + step_y + ny, ny))

    barrier = pltpu.get_barrier_semaphore()
    peers_x = [(at, my) for at in others(mx, SPLIT_X)]
    peers_y = [(mx, at) for at in others(my, SPLIT_Y)]
    peers = [there(sx, sy) for sx, sy in WAYS[4:]] + peers_x[::-1] + peers_y[::-1]
    loads = [pltpu.make_async_copy(src, dst, load_sem.at[n]) for n, (src, dst) in enumerate(zip(given, here))]
    loads[0].start()
    for peer in peers:
        pl.semaphore_signal(barrier, inc=1, device_id=peer, device_id_type=MESH)
    for n in LOAD_ORDER[1:]:
        loads[n].start()
    loads[0].wait()

    lane = iota((ROWS, COLS), 1)
    group = lane // 32
    low = lane % 32 < 16
    own = [[vel[l, c].astype(F32) for c in range(2)] for l in range(LEVELS)]
    for c in range(2):
        packed = None
        for l in range(LEVELS):
            first = own[l][c] if l == 0 else shift_lanes(own[l][c], 32 * l)
            last = own[l][c] if l == 3 else shift_lanes(own[l][c], 32 * (l + 1))
            both = jnp.where(low, first, last)
            packed = both if l == 0 else jnp.where(group == l, both, packed)
        v_cols[pl.ds(16 * c, 16), :] = packed.astype(BF16)
        if c == 0:
            packed_first = packed
    for side in range(2):
        cut = slice(8, 16) if side == 0 else slice(0, 8)
        rows = jnp.concatenate([own[l][c][cut] for l in range(LEVELS) for c in range(2)], axis=0)
        v_rows[side] = rows.astype(BF16)
        v_corner[side] = jnp.concatenate([packed_first[cut], packed[cut]], axis=0).astype(BF16)

    pl.semaphore_wait(barrier, len(peers))

    copies_v, copies_s = [], []
    for d in SEND_ORDER:
        sx, sy = WAYS[d]
        side = 0 if sy == 1 else 1
        if sy == 0:
            src, dst = v_cols, rv_cols.at[d]
        elif sx == 0:
            src, dst = v_rows.at[side], rv_rows.at[d - 2]
        else:
            src, dst = v_corner.at[side], rv_corner.at[d - 4]
        copy = pltpu.make_async_remote_copy(
            src_ref=src,
            dst_ref=dst,
            send_sem=v_send.at[d],
            recv_sem=v_recv.at[d],
            device_id=there(sx, sy),
            device_id_type=MESH,
        )
        copy.start()
        copies_v.append(copy)
    for n in LOAD_ORDER[5:]:
        loads[n].wait()
    w1pad[...] = jnp.zeros_like(w1pad)
    for dy in range(5):
        for dx in range(5):
            taps = w1[dy, dx].astype(F32)
            for c in range(2):
                w1pad[dx, c, pl.ds(10 + dy, 1), pl.ds(0, 128)] = taps[c : c + 1]
                w1pad[dx, c, pl.ds(11 + dy, 1), pl.ds(128, 128)] = taps[c : c + 1]
    for s in range(6):
        for dx in range(5):
            for c in range(2):
                block = w1pad[dx, c, pl.ds(10 - 2 * s, 16), :]
                w1all[s, pl.ds(32 * dx + 16 * c, 16), :] = block.astype(BF16)
        w1all[s, pl.ds(160, 96), :] = jnp.zeros((96, 256), BF16)

    kept = [d1[pl.ds(m, 1), :].astype(F32).astype(BF16) for m in range(2)]
    nothing = jnp.zeros((64, 128), BF16)
    for dy in range(-1, 6):
        if 0 <= dy < 5:
            g = [w2[dy, dx].astype(F32) for dx in range(5)]
            mixes = [g[0], g[3], g[2], g[4], (g[0] + g[1] + g[2]) * 0.5, g[3] + g[4], (g[0] - g[1] + g[2]) * 0.5]
            mixes = [mix.astype(BF16) for mix in mixes]
        for n in range(7):
            for m in range(2):
                block = mixes[n] * kept[m] if 0 <= dy < 5 else nothing
                for b in range(2):
                    if 0 <= dy + b < 6:
                        o, a = divmod(dy + b, 2)
                        w2all[pl.ds(128 * b + 64 * m, 64), pl.ds(((n * 3 + o) * 2 + a) * 128, 128)] = block

    w3f[...] = jnp.zeros_like(w3f)
    for ky in range(3):
        for dx in range(3):
            taps = w3[ky, dx].astype(F32) * 0.5
            for c in range(2):
                tap = taps[c : c + 1]
                both = jnp.concatenate([tap, tap], axis=1)
                for b in range(2):
                    w3f[pl.ds(8 * dx + 2 * (b + 2 - ky) + c, 1), pl.ds(128 * b, 128)] = both

    r = iota((M_V, 128), 0)
    lev = (r // 4) % 4
    x = 32 * (r % 4) + r // 16 - 5
    spot = jnp.where(x < 0, 512 + 32 * lev + 32 + x, jnp.where(x < 128, 128 * lev + x, 384 + 32 * lev + x))
    for k in range(5):
        pick[:, pl.ds(128 * k, 128)] = jnp.where(iota((M_V, 128), 1) + 128 * k == spot, 1.0, 0.0).astype(BF16)
    r = iota((512, 128), 0)
    spot = 128 * ((r // 4) % 4) + 32 * (r % 4) + r // 16
    for k in range(4):
        perm[:, pl.ds(128 * k, 128)] = jnp.where(iota((512, 128), 1) + 128 * k == spot, 1.0, 0.0).astype(BF16)

    for n in LOAD_ORDER[1:5]:
        loads[n].wait()
    st_own[0] = eta[...]
    st_own[1] = face[0]
    st_own[2] = face[1]
    st_own[3] = stor[...]
    st_own[4] = ocean[...].astype(F32)
    for d in SEND_ORDER:
        sx, sy = WAYS[d]
        if sy == 0:
            src, dst = st_own, rst_cols.at[d]
        else:
            src = st_own.at[:, pl.ds(8 if sy == 1 else 0, 8), :]
            dst = rst_rows.at[d - 2]
        copy = pltpu.make_async_remote_copy(
            src_ref=src,
            dst_ref=dst,
            send_sem=s_send.at[d],
            recv_sem=s_recv.at[d],
            device_id=there(sx, sy),
            device_id_type=MESH,
        )
        copy.start()
        copies_s.append(copy)

    has_south = jnp.where(my > 0, 1.0, 0.0)
    has_north = jnp.where(my < ny - 1, 1.0, 0.0)
    for copy in copies_v:
        copy.wait_recv()
    low8 = low[:8]
    south = rv_rows[0].astype(F32) * has_south
    north = rv_rows[1].astype(F32) * has_north
    from_w, from_e = rv_cols[0].astype(F32), rv_cols[1].astype(F32)
    from_sw, from_se = rv_corner[0].astype(F32), rv_corner[1].astype(F32)
    from_nw, from_ne = rv_corner[2].astype(F32), rv_corner[3].astype(F32)
    for c in range(2):
        for l in range(LEVELS):
            at = 8 * (2 * l + c)
            vx[l, c, pl.ds(0, 8), :] = south[at : at + 8]
            vx[l, c, pl.ds(8, 16), :] = own[l][c]
            vx[l, c, pl.ds(24, 8), :] = north[at : at + 8]
        cut = slice(8 * c, 8 * c + 8)
        vx[4, c, pl.ds(0, 8), :] = jnp.where(low8, from_se[cut], from_sw[cut]) * has_south
        cut16 = slice(16 * c, 16 * c + 16)
        vx[4, c, pl.ds(8, 16), :] = jnp.where(low, from_e[cut16], from_w[cut16])
        vx[4, c, pl.ds(24, 8), :] = jnp.where(low8, from_ne[cut], from_nw[cut]) * has_north
    for w in range(2):
        for k in range(5):
            for c in range(2):
                block = vx[k, c, pl.ds(3 + 10 * w, 16), :].astype(BF16)
                for rep in range(4):
                    bmat[pl.ds(128 * w + 32 * rep + 16 * c, 16), pl.ds(128 * k, 128)] = block
    umat[...] = dot_t(pick[...], bmat[...]).astype(BF16)

    bias1 = jnp.concatenate([b1[...].reshape(1, 128)] * 2, axis=1)
    upper = iota((1, 256), 1) // 128
    group1 = iota((M_1, 128), 1) // 32
    for w in range(2):
        lanes = pl.ds(128 * w, 128)
        near = umat[pl.ds(0, M_1), lanes]
        for g in range(1, 4):
            near = jnp.where(group1 == g, umat[pl.ds(16 * g, M_1), lanes], near)
        wide = jnp.concatenate([near, umat[pl.ds(64, M_1), lanes]], axis=1)

        for j in range(6 * w, 6 + 5 * w):
            acc = dot(wide, w1all[j - 5 * w])
            row = my * ROWS + 2 * j - 3 + upper
            scale = jnp.where((row >= 0) & (row < ny * ROWS), KEEP_SCALE, 0.0)
            hidden = (jnp.maximum(acc + bias1, 0.0) * scale).astype(BF16)
            h1[j] = hidden.reshape(XO_1 // 2, 32, 256)
            d = [h1[j, pl.ds(k // 2, U_2), pl.ds(16 * (k % 2), 16), :] for k in range(6)]
            mixes = (d[0] - d[2], d[3] - d[4], d[3] - d[1], d[5] - d[4], d[1] + d[2], d[2] - d[1])
            for n, mix in enumerate(mixes):
                mixed1[n, j] = mix

    bias2 = jnp.concatenate([b2[...].reshape(1, 64)] * 4, axis=1)
    keep2 = d2[...].astype(F32) * KEEP_SCALE
    keep2 = jnp.concatenate([keep2[0:1], keep2[1:2]] * 2, axis=1)
    w3all = w3f[...].astype(BF16)

    def layer_two(first, spans):
        def product(n):
            total = None
            for o in range(3):
                lefts = []
                for start, length in spans:
                    if n == 5:
                        left = h1[pl.ds(first + o, 3), pl.ds(start + 2, length), pl.ds(0, 16), :]
                    else:
                        left = mixed1[min(n, 5), pl.ds(first + o, 3), pl.ds(start, length), :, :]
                    lefts.append(left.reshape(48 * length, 256))
                left = lefts[0] if len(lefts) == 1 else jnp.concatenate(lefts, axis=0)
                term = dot_t(left, w2all[:, pl.ds((n * 3 + o) * 256, 256)])
                total = term if total is None else total + term
            return total

        both = product(4) + product(5)
        half = product(6)
        even = product(0) + product(1) + (both + half)
        odd = product(2) + product(3) + (both - half)
        at = 0
        for start, length in spans:
            for q in range(3):
                row = my * ROWS + 2 * (first + q) - 1 + upper
                scale = jnp.where((row >= 0) & (row < ny * ROWS), keep2, 0.0)
                for e, acc in enumerate((even, odd)):
                    hidden = jnp.maximum(acc[at : at + 16 * length] + bias2, 0.0) * scale
                    h2[first + q, pl.ds(start, length), pl.ds(16 * e, 16), :] = hidden.astype(BF16).reshape(length, 16, 256)
                at += 16 * length

    def layer_three(first):
        for i in range(first, first + 3):
            z = dot_t(w3all, h2[i].reshape(M_2, 256))
            zacc[i] = z[0:8, 0:512] + z[8:16, 16:528] + z[16:24, 32:544]

    def finish(fx, f):
        mixed = jnp.concatenate([zacc[p, pl.ds(4, 4), :] + zacc[p + 1, pl.ds(0, 4), :] for p in range(8)], axis=0)
        high = mixed.astype(BF16)
        rest = (mixed - high.astype(F32)).astype(BF16)
        out = dot(jnp.concatenate([high, rest], axis=0), perm[...])
        for l in range(LEVELS):
            lanes = slice(128 * l, 128 * l + 128)
            mixed_out[l] = out[0:32, lanes] + out[32:64, lanes]
        for c in range(2):
            total = None
            for l in range(LEVELS):
                forcing = mixed_out[l, pl.ds(c, 16, stride=2), :] + b3[c]
                if f is not None:
                    f[l, c] = forcing
                term = thick[l] * (vel[l, c].astype(F32) + forcing)
                total = term if total is None else total + term
            fx[c] = total

    def outer_rows(n, carry):
        layer_two(6 * n, [(0, U_2)])
        return carry

    lax.fori_loop(0, 2, outer_rows, 0)
    h2[pl.ds(3, 3), pl.ds(EDGE_W, EDGE_E - EDGE_W), :, :] = jnp.zeros((3, EDGE_E - EDGE_W, 32, 256), BF16)
    layer_two(3, [(0, EDGE_W), (EDGE_E, U_2 - EDGE_E)])
    layer_three(0)
    layer_three(6)
    layer_three(3)
    finish(fx_own, None)

    copies_x = []
    for d in SEND_ORDER:
        sx, sy = WAYS[d]
        if sy == 0:
            src, dst = fx_own, rfx_cols.at[d]
        else:
            src = fx_own.at[:, pl.ds(8 if sy == 1 else 0, 8), :]
            dst = rfx_rows.at[d - 2]
        copy = pltpu.make_async_remote_copy(
            src_ref=src,
            dst_ref=dst,
            send_sem=x_send.at[d],
            recv_sem=x_recv.at[d],
            device_id=there(sx, sy),
            device_id_type=MESH,
        )
        copy.start()
        copies_x.append(copy)

    layer_two(3, [(EDGE_W, EDGE_E - EDGE_W)])
    layer_three(3)
    finish(fx_all, f_out)

    for copy in copies_s:
        copy.wait_recv()

    side = iota((ROWS, COLS), 1) < 64
    side8 = side[:8]

    def widened(own_ref, cols_ref, rows_ref, k):
        middle = jnp.concatenate([own_ref[k], jnp.where(side, cols_ref[1, k], cols_ref[0, k])], axis=1)
        below = jnp.concatenate([rows_ref[0, k], jnp.where(side8, rows_ref[3, k], rows_ref[2, k])], axis=1)
        above = jnp.concatenate([rows_ref[1, k], jnp.where(side8, rows_ref[5, k], rows_ref[4, k])], axis=1)
        return jnp.concatenate([below, middle, above], axis=0)

    eta_w, east_w, north_w, stor_w, sea = [widened(st_own, rst_cols, rst_rows, k) for k in range(5)]
    place = iota(sea.shape, 0) - 8 + my * ROWS
    sea = jnp.where((place >= 0) & (place < ny * ROWS), sea, 0.0)
    open_east = sea * shift_lanes(sea, -1)
    open_north = sea * shift_rows(sea, -1)
    coef_east = east_w * open_east
    coef_north = north_w * open_north
    coef_west = shift_lanes(coef_east, 1)
    coef_south = shift_rows(coef_north, 1)
    diagonal = stor_w + coef_east + coef_west + coef_north + coef_south

    def operate(field):
        return (
            diagonal * field
            - coef_east * shift_lanes(field, -1)
            - coef_west * shift_lanes(field, 1)
            - coef_north * shift_rows(field, -1)
            - coef_south * shift_rows(field, 1)
        )

    known = stor_w * eta_w - operate(eta_w)
    for copy in copies_x:
        copy.wait_recv()
    zonal, merid = [widened(fx_all, rfx_cols, rfx_rows, k) for k in range(2)]
    flux_east = zonal * open_east
    flux_north = merid * open_north
    diverge = flux_east - shift_lanes(flux_east, 1) + flux_north - shift_rows(flux_north, 1)
    k0 = known - diverge
    k1 = operate(k0)
    k2 = operate(k1)
    k3 = operate(k2)
    k0, k1, k2, k3 = [k[8:24, 0:128] for k in (k0, k1, k2, k3)]

    lane1 = iota((1, 128), 1)
    sums = jnp.zeros((1, 128), F32)
    for n, (a, b) in enumerate(((k0, k0), (k0, k1), (k1, k1), (k1, k2), (k2, k2), (k2, k3))):
        total = jnp.sum(jnp.sum(a * b, axis=0, keepdims=True), axis=1, keepdims=True)
        sums = jnp.where(lane1 == n, total, sums)

    def exchange(values, mine, got, send, recv, targets):
        mine[...] = values
        copies = []
        for k, target in enumerate(targets):
            copy = pltpu.make_async_remote_copy(
                src_ref=mine,
                dst_ref=got.at[k],
                send_sem=send.at[k],
                recv_sem=recv.at[k],
                device_id=target,
                device_id_type=MESH,
            )
            copy.start()
            copies.append(copy)
        for copy in copies:
            copy.wait_recv()
        return values + jnp.sum(got[...], axis=0), copies

    sums, copies_a = exchange(sums, red_a, got_a, a_send, a_recv, peers_x)
    sums, copies_b = exchange(sums, red_b, got_b, b_send, b_recv, peers_y)
    m0, m1, m2, m3, m4, m5 = [
        jnp.sum(jnp.where(lane1 == n, sums, 0.0), axis=1, keepdims=True) for n in range(6)
    ]

    def over(value, scale):
        fine = value > 1e-6 * scale
        return jnp.where(fine, 1.0 / jnp.where(fine, value, 1.0), 0.0)

    inv0 = over(m1, jnp.zeros_like(m1))
    l1 = m2 * inv0
    l2 = m3 * inv0
    p1 = m3 - l1 * m2
    inv1 = over(p1, m3)
    e21 = m4 - l2 * m2
    l21 = e21 * inv1
    p2 = m5 - l2 * m3 - l21 * e21
    inv2 = jnp.where(inv1 > 0.0, over(p2, m5), 0.0)
    z1 = m1 - l1 * m0
    z2 = m2 - l2 * m0 - l21 * z1
    c2 = z2 * inv2
    c1 = z1 * inv1 - l21 * c2
    c0 = m0 * inv0 - l1 * c1 - l2 * c2
    e_out[...] = eta[...] + c0 * k0 + c1 * k1 + c2 * k2

    for copy in copies_v + copies_s + copies_x + copies_a + copies_b:
        copy.wait_send()


def body(nx, ny, *args):
    vmem = pl.BlockSpec(memory_space=pltpu.VMEM)
    args = list(args)
    args[1] = jnp.transpose(args[1], (1, 2, 0, 3))
    args[5] = jnp.transpose(args[5], (1, 2, 0, 3))
    here = [(pltpu.SMEM if n in (6, 9) else pltpu.VMEM)(a.shape, a.dtype) for n, a in enumerate(args)]
    dma = pltpu.SemaphoreType.DMA
    V = pltpu.VMEM
    return pl.pallas_call(
        functools.partial(kernel, nx, ny),
        out_shape=(
            pltpu.VMEM((LEVELS, 2, ROWS, COLS), F32),
            pltpu.VMEM((ROWS, COLS), F32),
        ),
        in_specs=[pl.BlockSpec(memory_space=pltpu.HBM)] * 14,
        out_specs=(vmem, vmem),
        scratch_shapes=here + [
            V((2, 64, 128), BF16),
            V((32, 128), BF16),
            V((2, 16, 128), BF16),
            V((5, ROWS, COLS), F32),
            V((2, ROWS, COLS), F32),
            V((2, ROWS, COLS), F32),
            V((2, 64, 128), BF16),
            V((2, 32, 128), BF16),
            V((4, 16, 128), BF16),
            V((2, 5, ROWS, COLS), F32),
            V((6, 5, 8, COLS), F32),
            V((2, 2, ROWS, COLS), F32),
            V((6, 2, 8, COLS), F32),
            V((1, 128), F32),
            V((1, 128), F32),
            V((nx - 1, 1, 128), F32),
            V((ny - 1, 1, 128), F32),
            V((5, 2, 32, 128), F32),
            V((256, 640), BF16),
            V((M_V, 640), BF16),
            V((M_V, 256), BF16),
            V((5, 2, 32, 256), F32),
            V((6, 256, 256), BF16),
            V((256, 7 * 768), BF16),
            V((32, 256), F32),
            V((11, XO_1 // 2, 32, 256), BF16),
            V((6, 11, U_2, 16, 256), BF16),
            V((9, U_2, 32, 256), BF16),
            V((9, 8, 512), F32),
            V((LEVELS, 32, 128), F32),
            V((512, 512), BF16),
            dma((8,)),
            dma((8,)),
            dma((8,)),
            dma((8,)),
            dma((8,)),
            dma((8,)),
            dma((nx - 1,)),
            dma((nx - 1,)),
            dma((ny - 1,)),
            dma((ny - 1,)),
            dma((14,)),
        ],
        compiler_params=pltpu.CompilerParams(
            collective_id=0, has_side_effects=True, vmem_limit_bytes=60 * 2**20
        ),
        name="ocean_step",
    )(*args)


def solution(mesh):
    nx, ny = mesh.shape["gx"], mesh.shape["gy"]
    tile = P("gy", "gx")
    stacked = P(None, "gy", "gx")
    levels = P(None, None, "gy", "gx")
    in_specs = (levels,) + (P(),) * 9 + (tile, stacked, tile, tile)
    return jax.shard_map(
        functools.partial(body, nx, ny),
        mesh=mesh,
        in_specs=in_specs,
        out_specs=(levels, tile),
        check_vma=False,
    )
```

```python
import functools
import itertools

import jax
import jax.numpy as jnp
from jax import lax
from jax.experimental import pallas as pl
from jax.experimental.pallas import tpu as pltpu
from jax.sharding import PartitionSpec as P

MESH = pl.DeviceIdType.MESH
F32 = jnp.float32
BF16 = jnp.bfloat16
KEEP_SCALE = 4.0 / 3.0

WAYS = ((1, 0), (-1, 0), (0, 1), (0, -1), (1, 1), (-1, 1), (1, -1), (-1, -1))

ROWS, COLS, LEVELS = 16, 128, 4
SEND_ORDER = (4, 5, 6, 7, 2, 3, 0, 1)

SPLIT_X = ((2, 2), (4, 1), (2, 0))
SPLIT_Y = ((2, 1), (8, 1))

LOAD_ORDER = (0, 10, 11, 12, 13, 1, 7, 3, 5, 2, 4, 6, 8, 9)

XO_V, XO_1, XO_2 = 42, 38, 34
U_2 = XO_2 // 2
EDGE_W, EDGE_E = 3, 14
M_V, M_1, M_2 = 16 * XO_V, 16 * XO_1, 16 * XO_2


def iota(shape, dim):
    return lax.broadcasted_iota(jnp.int32, shape, dim)


def dot_t(a, b):
    return lax.dot_general(a, b, (((1,), (1,)), ((), ())), preferred_element_type=F32)


def dot(a, b):
    return jnp.dot(a, b, preferred_element_type=F32)


def others(index, split):
    sizes = [size for size, _ in split]
    steps = list(itertools.product(*[range(size) for size in sizes]))[1:]
    steps.sort(key=lambda step: -sum(hops * min(k, size - k) for k, (size, hops) in zip(step, split)))
    found = []
    for step in steps:
        at, stride = 0, 1
        for k, size in reversed(list(zip(step, sizes))):
            digit = lax.rem(lax.div(index, jnp.int32(stride)), jnp.int32(size))
            at = at + lax.rem(digit + k, jnp.int32(size)) * stride
            stride *= size
        found.append(at)
    return found


def shift_lanes(x, by):
    return pltpu.roll(x, by % x.shape[1], 1)


def shift_rows(x, by):
    return pltpu.roll(x, by % x.shape[0], 0)


def kernel(
    nx,
    ny,
    *refs,
):
    given, refs = refs[:14], refs[14:]
    (f_out, e_out), refs = refs[:2], refs[2:]
    here, refs = refs[:14], refs[14:]
    vel, w1, b1, w2, b2, w3, b3, d1, d2, thick, eta, face, stor, ocean = here
    (
        v_rows,
        v_cols,
        v_corner,
        st_own,
        fx_own,
        fx_all,
        rv_rows,
        rv_cols,
        rv_corner,
        rst_cols,
        rst_rows,
        rfx_cols,
        rfx_rows,
        red_a,
        red_b,
        got_a,
        got_b,
        vx,
        bmat,
        pick,
        umat,
        w1pad,
        w1all,
        w2all,
        w3f,
        h1,
        mixed1,
        h2,
        zacc,
        mixed_out,
        perm,
        v_send,
        v_recv,
        s_send,
        s_recv,
        x_send,
        x_recv,
        a_send,
        a_recv,
        b_send,
        b_recv,
        load_sem,
    ) = refs
    mx = lax.axis_index("gx")
    my = lax.axis_index("gy")

    def there(step_x, step_y):
        return (lax.rem(mx + step_x + nx, nx), lax.rem(my + step_y + ny, ny))

    barrier = pltpu.get_barrier_semaphore()
    peers_x = [(at, my) for at in others(mx, SPLIT_X)]
    peers_y = [(mx, at) for at in others(my, SPLIT_Y)]
    peers = [there(sx, sy) for sx, sy in WAYS[4:]] + peers_x[::-1] + peers_y[::-1]
    loads = [pltpu.make_async_copy(src, dst, load_sem.at[n]) for n, (src, dst) in enumerate(zip(given, here))]
    loads[0].start()
    for peer in peers:
        pl.semaphore_signal(barrier, inc=1, device_id=peer, device_id_type=MESH)
    for n in LOAD_ORDER[1:]:
        loads[n].start()
    loads[0].wait()

    lane = iota((ROWS, COLS), 1)
    group = lane // 32
    low = lane % 32 < 16
    own = [[vel[l, c].astype(F32) for c in range(2)] for l in range(LEVELS)]
    for c in range(2):
        packed = None
        for l in range(LEVELS):
            first = own[l][c] if l == 0 else shift_lanes(own[l][c], 32 * l)
            last = own[l][c] if l == 3 else shift_lanes(own[l][c], 32 * (l + 1))
            both = jnp.where(low, first, last)
            packed = both if l == 0 else jnp.where(group == l, both, packed)
        v_cols[pl.ds(16 * c, 16), :] = packed.astype(BF16)
        if c == 0:
            packed_first = packed
    for side in range(2):
        cut = slice(8, 16) if side == 0 else slice(0, 8)
        rows = jnp.concatenate([own[l][c][cut] for l in range(LEVELS) for c in range(2)], axis=0)
        v_rows[side] = rows.astype(BF16)
        v_corner[side] = jnp.concatenate([packed_first[cut], packed[cut]], axis=0).astype(BF16)

    pl.semaphore_wait(barrier, len(peers))

    copies_v, copies_s = [], []
    for d in SEND_ORDER:
        sx, sy = WAYS[d]
        side = 0 if sy == 1 else 1
        if sy == 0:
            src, dst = v_cols, rv_cols.at[d]
        elif sx == 0:
            src, dst = v_rows.at[side], rv_rows.at[d - 2]
        else:
            src, dst = v_corner.at[side], rv_corner.at[d - 4]
        copy = pltpu.make_async_remote_copy(
            src_ref=src,
            dst_ref=dst,
            send_sem=v_send.at[d],
            recv_sem=v_recv.at[d],
            device_id=there(sx, sy),
            device_id_type=MESH,
        )
        copy.start()
        copies_v.append(copy)
    for n in LOAD_ORDER[5:]:
        loads[n].wait()
    w1pad[...] = jnp.zeros_like(w1pad)
    for dy in range(5):
        for dx in range(5):
            taps = w1[dy, dx].astype(F32)
            for c in range(2):
                w1pad[dx, c, pl.ds(10 + dy, 1), pl.ds(0, 128)] = taps[c : c + 1]
                w1pad[dx, c, pl.ds(11 + dy, 1), pl.ds(128, 128)] = taps[c : c + 1]
    for s in range(6):
        for dx in range(5):
            for c in range(2):
                block = w1pad[dx, c, pl.ds(10 - 2 * s, 16), :]
                w1all[s, pl.ds(32 * dx + 16 * c, 16), :] = block.astype(BF16)
        w1all[s, pl.ds(160, 96), :] = jnp.zeros((96, 256), BF16)

    kept = [d1[pl.ds(m, 1), :].astype(F32).astype(BF16) for m in range(2)]
    nothing = jnp.zeros((64, 128), BF16)
    left4 = left5 = jnp.zeros((64, 128), F32)
    for dy in range(-1, 6):
        if 0 <= dy < 5:
            g = [w2[dy, dx].astype(F32) for dx in range(5)]
            sum4 = (g[0] + g[1] + g[2]) * 0.5 + left4
            sum5 = g[3] + g[4] + left5
            mixes = [g[0], g[3], g[2], g[4], sum4, sum5, (g[0] - g[1] + g[2]) * 0.5]
            mixes = [mix.astype(BF16) for mix in mixes]
            left4 = sum4 - mixes[4].astype(F32)
            left5 = sum5 - mixes[5].astype(F32)
        for n in range(7):
            for m in range(2):
                block = mixes[n] * kept[m] if 0 <= dy < 5 else nothing
                for b in range(2):
                    if 0 <= dy + b < 6:
                        o, a = divmod(dy + b, 2)
                        w2all[pl.ds(128 * b + 64 * m, 64), pl.ds(((n * 3 + o) * 2 + a) * 128, 128)] = block

    w3f[...] = jnp.zeros_like(w3f)
    for ky in range(3):
        for dx in range(3):
            taps = w3[ky, dx].astype(F32) * 0.5
            for c in range(2):
                tap = taps[c : c + 1]
                both = jnp.concatenate([tap, tap], axis=1)
                for b in range(2):
                    w3f[pl.ds(8 * dx + 2 * (b + 2 - ky) + c, 1), pl.ds(128 * b, 128)] = both

    r = iota((M_V, 128), 0)
    lev = (r // 4) % 4
    x = 32 * (r % 4) + r // 16 - 5
    spot = jnp.where(x < 0, 512 + 32 * lev + 32 + x, jnp.where(x < 128, 128 * lev + x, 384 + 32 * lev + x))
    for k in range(5):
        pick[:, pl.ds(128 * k, 128)] = jnp.where(iota((M_V, 128), 1) + 128 * k == spot, 1.0, 0.0).astype(BF16)
    r = iota((512, 128), 0)
    spot = 128 * ((r // 4) % 4) + 32 * (r % 4) + r // 16
    for k in range(4):
        perm[:, pl.ds(128 * k, 128)] = jnp.where(iota((512, 128), 1) + 128 * k == spot, 1.0, 0.0).astype(BF16)

    for n in LOAD_ORDER[1:5]:
        loads[n].wait()
    st_own[0] = eta[...]
    st_own[1] = face[0]
    st_own[2] = face[1]
    st_own[3] = stor[...]
    st_own[4] = ocean[...].astype(F32)
    for d in SEND_ORDER:
        sx, sy = WAYS[d]
        if sy == 0:
            src, dst = st_own, rst_cols.at[d]
        else:
            src = st_own.at[:, pl.ds(8 if sy == 1 else 0, 8), :]
            dst = rst_rows.at[d - 2]
        copy = pltpu.make_async_remote_copy(
            src_ref=src,
            dst_ref=dst,
            send_sem=s_send.at[d],
            recv_sem=s_recv.at[d],
            device_id=there(sx, sy),
            device_id_type=MESH,
        )
        copy.start()
        copies_s.append(copy)

    has_south = jnp.where(my > 0, 1.0, 0.0)
    has_north = jnp.where(my < ny - 1, 1.0, 0.0)
    for copy in copies_v:
        copy.wait_recv()
    low8 = low[:8]
    south = rv_rows[0].astype(F32) * has_south
    north = rv_rows[1].astype(F32) * has_north
    from_w, from_e = rv_cols[0].astype(F32), rv_cols[1].astype(F32)
    from_sw, from_se = rv_corner[0].astype(F32), rv_corner[1].astype(F32)
    from_nw, from_ne = rv_corner[2].astype(F32), rv_corner[3].astype(F32)
    for c in range(2):
        for l in range(LEVELS):
            at = 8 * (2 * l + c)
            vx[l, c, pl.ds(0, 8), :] = south[at : at + 8]
            vx[l, c, pl.ds(8, 16), :] = own[l][c]
            vx[l, c, pl.ds(24, 8), :] = north[at : at + 8]
        cut = slice(8 * c, 8 * c + 8)
        vx[4, c, pl.ds(0, 8), :] = jnp.where(low8, from_se[cut], from_sw[cut]) * has_south
        cut16 = slice(16 * c, 16 * c + 16)
        vx[4, c, pl.ds(8, 16), :] = jnp.where(low, from_e[cut16], from_w[cut16])
        vx[4, c, pl.ds(24, 8), :] = jnp.where(low8, from_ne[cut], from_nw[cut]) * has_north
    for w in range(2):
        for k in range(5):
            for c in range(2):
                block = vx[k, c, pl.ds(3 + 10 * w, 16), :].astype(BF16)
                for rep in range(4):
                    bmat[pl.ds(128 * w + 32 * rep + 16 * c, 16), pl.ds(128 * k, 128)] = block
    umat[...] = dot_t(pick[...], bmat[...]).astype(BF16)

    bias1 = jnp.concatenate([b1[...].reshape(1, 128)] * 2, axis=1)
    upper = iota((1, 256), 1) // 128
    group1 = iota((M_1, 128), 1) // 32
    for w in range(2):
        lanes = pl.ds(128 * w, 128)
        near = umat[pl.ds(0, M_1), lanes]
        for g in range(1, 4):
            near = jnp.where(group1 == g, umat[pl.ds(16 * g, M_1), lanes], near)
        wide = jnp.concatenate([near, umat[pl.ds(64, M_1), lanes]], axis=1)

        for j in range(6 * w, 6 + 5 * w):
            acc = dot(wide, w1all[j - 5 * w])
            row = my * ROWS + 2 * j - 3 + upper
            scale = jnp.where((row >= 0) & (row < ny * ROWS), KEEP_SCALE, 0.0)
            hidden = (jnp.maximum(acc + bias1, 0.0) * scale).astype(BF16)
            h1[j] = hidden.reshape(XO_1 // 2, 32, 256)
            d = [h1[j, pl.ds(k // 2, U_2), pl.ds(16 * (k % 2), 16), :] for k in range(6)]
            mixes = (d[0] - d[2], d[3] - d[4], d[3] - d[1], d[5] - d[4], d[1] + d[2], d[2] - d[1])
            for n, mix in enumerate(mixes):
                mixed1[n, j] = mix

    bias2 = jnp.concatenate([b2[...].reshape(1, 64)] * 4, axis=1)
    keep2 = d2[...].astype(F32) * KEEP_SCALE
    keep2 = jnp.concatenate([keep2[0:1], keep2[1:2]] * 2, axis=1)
    w3all = w3f[...].astype(BF16)

    def layer_two(first, spans):
        def product(*which):
            total = None
            for n, o in itertools.product(which, range(3)):
                lefts = []
                for start, length in spans:
                    if n == 5:
                        left = h1[pl.ds(first + o, 3), pl.ds(start + 2, length), pl.ds(0, 16), :]
                    else:
                        left = mixed1[min(n, 5), pl.ds(first + o, 3), pl.ds(start, length), :, :]
                    lefts.append(left.reshape(48 * length, 256))
                left = lefts[0] if len(lefts) == 1 else jnp.concatenate(lefts, axis=0)
                term = dot_t(left, w2all[:, pl.ds((n * 3 + o) * 256, 256)])
                total = term if total is None else total + term
            return total

        both, half = product(4, 5), product(6)
        even = product(0, 1) + (both + half)
        odd = product(2, 3) + (both - half)
        at = 0
        for start, length in spans:
            for q in range(3):
                row = my * ROWS + 2 * (first + q) - 1 + upper
                scale = jnp.where((row >= 0) & (row < ny * ROWS), keep2, 0.0)
                for e, acc in enumerate((even, odd)):
                    hidden = jnp.maximum(acc[at : at + 16 * length] + bias2, 0.0) * scale
                    h2[first + q, pl.ds(start, length), pl.ds(16 * e, 16), :] = hidden.astype(BF16).reshape(length, 16, 256)
                at += 16 * length

    def layer_three(first):
        for i in range(first, first + 3):
            z = dot_t(w3all, h2[i].reshape(M_2, 256))
            zacc[i] = z[0:8, 0:512] + z[8:16, 16:528] + z[16:24, 32:544]

    def finish(fx, f):
        mixed = jnp.concatenate([zacc[p, pl.ds(4, 4), :] + zacc[p + 1, pl.ds(0, 4), :] for p in range(8)], axis=0)
        high = mixed.astype(BF16)
        rest = (mixed - high.astype(F32)).astype(BF16)
        out = dot(jnp.concatenate([high, rest], axis=0), perm[...])
        for l in range(LEVELS):
            lanes = slice(128 * l, 128 * l + 128)
            mixed_out[l] = out[0:32, lanes] + out[32:64, lanes]
        for c in range(2):
            total = None
            for l in range(LEVELS):
                forcing = mixed_out[l, pl.ds(c, 16, stride=2), :] + b3[c]
                if f is not None:
                    f[l, c] = forcing
                term = thick[l] * (vel[l, c].astype(F32) + forcing)
                total = term if total is None else total + term
            fx[c] = total

    layer_two(0, [(0, U_2)])
    layer_two(6, [(0, U_2)])
    h2[pl.ds(3, 3), pl.ds(EDGE_W, EDGE_E - EDGE_W), :, :] = jnp.zeros((3, EDGE_E - EDGE_W, 32, 256), BF16)
    layer_two(3, [(0, EDGE_W), (EDGE_E, U_2 - EDGE_E)])
    layer_three(0)
    layer_three(6)
    layer_three(3)
    finish(fx_own, None)

    copies_x = []
    for d in SEND_ORDER:
        sx, sy = WAYS[d]
        if sy == 0:
            src, dst = fx_own, rfx_cols.at[d]
        else:
            src = fx_own.at[:, pl.ds(8 if sy == 1 else 0, 8), :]
            dst = rfx_rows.at[d - 2]
        copy = pltpu.make_async_remote_copy(
            src_ref=src,
            dst_ref=dst,
            send_sem=x_send.at[d],
            recv_sem=x_recv.at[d],
            device_id=there(sx, sy),
            device_id_type=MESH,
        )
        copy.start()
        copies_x.append(copy)

    layer_two(3, [(EDGE_W, EDGE_E - EDGE_W)])
    layer_three(3)
    finish(fx_all, f_out)

    for copy in copies_s:
        copy.wait_recv()

    side = iota((ROWS, COLS), 1) < 64
    side8 = side[:8]

    def widened(own_ref, cols_ref, rows_ref, k):
        middle = jnp.concatenate([own_ref[k], jnp.where(side, cols_ref[1, k], cols_ref[0, k])], axis=1)
        below = jnp.concatenate([rows_ref[0, k], jnp.where(side8, rows_ref[3, k], rows_ref[2, k])], axis=1)
        above = jnp.concatenate([rows_ref[1, k], jnp.where(side8, rows_ref[5, k], rows_ref[4, k])], axis=1)
        return jnp.concatenate([below, middle, above], axis=0)

    eta_w, east_w, north_w, stor_w, sea = [widened(st_own, rst_cols, rst_rows, k) for k in range(5)]
    place = iota(sea.shape, 0) - 8 + my * ROWS
    sea = jnp.where((place >= 0) & (place < ny * ROWS), sea, 0.0)
    open_east = sea * shift_lanes(sea, -1)
    open_north = sea * shift_rows(sea, -1)
    coef_east = east_w * open_east
    coef_north = north_w * open_north
    coef_west = shift_lanes(coef_east, 1)
    coef_south = shift_rows(coef_north, 1)
    diagonal = stor_w + coef_east + coef_west + coef_north + coef_south

    def operate(field):
        return (
            diagonal * field
            - coef_east * shift_lanes(field, -1)
            - coef_west * shift_lanes(field, 1)
            - coef_north * shift_rows(field, -1)
            - coef_south * shift_rows(field, 1)
        )

    known = stor_w * eta_w - operate(eta_w)
    for copy in copies_x:
        copy.wait_recv()
    zonal, merid = [widened(fx_all, rfx_cols, rfx_rows, k) for k in range(2)]
    flux_east = zonal * open_east
    flux_north = merid * open_north
    diverge = flux_east - shift_lanes(flux_east, 1) + flux_north - shift_rows(flux_north, 1)
    k0 = known - diverge
    k1 = operate(k0)
    k2 = operate(k1)
    k3 = operate(k2)
    k0, k1, k2, k3 = [k[8:24, 0:128] for k in (k0, k1, k2, k3)]

    lane1 = iota((1, 128), 1)
    sums = jnp.zeros((1, 128), F32)
    for n, (a, b) in enumerate(((k0, k0), (k0, k1), (k1, k1), (k1, k2), (k2, k2), (k2, k3))):
        total = jnp.sum(jnp.sum(a * b, axis=0, keepdims=True), axis=1, keepdims=True)
        sums = jnp.where(lane1 == n, total, sums)

    def exchange(values, mine, got, send, recv, targets):
        mine[...] = values
        copies = []
        for k, target in enumerate(targets):
            copy = pltpu.make_async_remote_copy(
                src_ref=mine,
                dst_ref=got.at[k],
                send_sem=send.at[k],
                recv_sem=recv.at[k],
                device_id=target,
                device_id_type=MESH,
            )
            copy.start()
            copies.append(copy)
        for copy in copies:
            copy.wait_recv()
        return values + jnp.sum(got[...], axis=0), copies

    sums, copies_a = exchange(sums, red_a, got_a, a_send, a_recv, peers_x)
    sums, copies_b = exchange(sums, red_b, got_b, b_send, b_recv, peers_y)
    m0, m1, m2, m3, m4, m5 = [
        jnp.sum(jnp.where(lane1 == n, sums, 0.0), axis=1, keepdims=True) for n in range(6)
    ]

    def over(value, scale):
        fine = value > 1e-6 * scale
        return jnp.where(fine, 1.0 / jnp.where(fine, value, 1.0), 0.0)

    inv0 = over(m1, jnp.zeros_like(m1))
    l1 = m2 * inv0
    l2 = m3 * inv0
    p1 = m3 - l1 * m2
    inv1 = over(p1, m3)
    e21 = m4 - l2 * m2
    l21 = e21 * inv1
    p2 = m5 - l2 * m3 - l21 * e21
    inv2 = jnp.where(inv1 > 0.0, over(p2, m5), 0.0)
    z1 = m1 - l1 * m0
    z2 = m2 - l2 * m0 - l21 * z1
    c2 = z2 * inv2
    c1 = z1 * inv1 - l21 * c2
    c0 = m0 * inv0 - l1 * c1 - l2 * c2
    e_out[...] = eta[...] + c0 * k0 + c1 * k1 + c2 * k2

    for copy in copies_v + copies_s + copies_x + copies_a + copies_b:
        copy.wait_send()


def body(nx, ny, *args):
    vmem = pl.BlockSpec(memory_space=pltpu.VMEM)
    args = list(args)
    args[1] = jnp.transpose(args[1], (1, 2, 0, 3))
    args[5] = jnp.transpose(args[5], (1, 2, 0, 3))
    here = [(pltpu.SMEM if n in (6, 9) else pltpu.VMEM)(a.shape, a.dtype) for n, a in enumerate(args)]
    dma = pltpu.SemaphoreType.DMA
    V = pltpu.VMEM
    return pl.pallas_call(
        functools.partial(kernel, nx, ny),
        out_shape=(
            pltpu.VMEM((LEVELS, 2, ROWS, COLS), F32),
            pltpu.VMEM((ROWS, COLS), F32),
        ),
        in_specs=[pl.BlockSpec(memory_space=pltpu.HBM)] * 14,
        out_specs=(vmem, vmem),
        scratch_shapes=here + [
            V((2, 64, 128), BF16),
            V((32, 128), BF16),
            V((2, 16, 128), BF16),
            V((5, ROWS, COLS), F32),
            V((2, ROWS, COLS), F32),
            V((2, ROWS, COLS), F32),
            V((2, 64, 128), BF16),
            V((2, 32, 128), BF16),
            V((4, 16, 128), BF16),
            V((2, 5, ROWS, COLS), F32),
            V((6, 5, 8, COLS), F32),
            V((2, 2, ROWS, COLS), F32),
            V((6, 2, 8, COLS), F32),
            V((1, 128), F32),
            V((1, 128), F32),
            V((nx - 1, 1, 128), F32),
            V((ny - 1, 1, 128), F32),
            V((5, 2, 32, 128), F32),
            V((256, 640), BF16),
            V((M_V, 640), BF16),
            V((M_V, 256), BF16),
            V((5, 2, 32, 256), F32),
            V((6, 256, 256), BF16),
            V((256, 7 * 768), BF16),
            V((32, 256), F32),
            V((11, XO_1 // 2, 32, 256), BF16),
            V((6, 11, U_2, 16, 256), BF16),
            V((9, U_2, 32, 256), BF16),
            V((9, 8, 512), F32),
            V((LEVELS, 32, 128), F32),
            V((512, 512), BF16),
            dma((8,)),
            dma((8,)),
            dma((8,)),
            dma((8,)),
            dma((8,)),
            dma((8,)),
            dma((nx - 1,)),
            dma((nx - 1,)),
            dma((ny - 1,)),
            dma((ny - 1,)),
            dma((14,)),
        ],
        compiler_params=pltpu.CompilerParams(
            collective_id=0, has_side_effects=True, vmem_limit_bytes=60 * 2**20
        ),
        name="ocean_step",
    )(*args)


def solution(mesh):
    nx, ny = mesh.shape["gx"], mesh.shape["gy"]
    tile = P("gy", "gx")
    stacked = P(None, "gy", "gx")
    levels = P(None, None, "gy", "gx")
    in_specs = (levels,) + (P(),) * 9 + (tile, stacked, tile, tile)
    return jax.shard_map(
        functools.partial(body, nx, ny),
        mesh=mesh,
        in_specs=in_specs,
        out_specs=(levels, tile),
        check_vma=False,
    )
```

```python
import functools
import itertools

import jax
import jax.numpy as jnp
from jax import lax
from jax.experimental import pallas as pl
from jax.experimental.pallas import tpu as pltpu
from jax.sharding import PartitionSpec as P

MESH = pl.DeviceIdType.MESH
F32 = jnp.float32
BF16 = jnp.bfloat16
KEEP_SCALE = 4.0 / 3.0

WAYS = ((1, 0), (-1, 0), (0, 1), (0, -1), (1, 1), (-1, 1), (1, -1), (-1, -1))

ROWS, COLS, LEVELS = 16, 128, 4
SEND_ORDER = (4, 5, 6, 7, 2, 3, 0, 1)

SPLIT_X = ((2, 2), (4, 1), (2, 0))
SPLIT_Y = ((2, 1), (8, 1))

LOAD_ORDER = (0, 10, 11, 12, 13, 1, 7, 3, 5, 2, 4, 6, 8, 9)

XO_V, XO_1, XO_2 = 42, 38, 34
U_2 = XO_2 // 2
EDGE_W, EDGE_E = 3, 14
M_V, M_1, M_2 = 16 * XO_V, 16 * XO_1, 16 * XO_2


def iota(shape, dim):
    return lax.broadcasted_iota(jnp.int32, shape, dim)


def dot_t(a, b):
    return lax.dot_general(a, b, (((1,), (1,)), ((), ())), preferred_element_type=F32)


def dot(a, b):
    return jnp.dot(a, b, preferred_element_type=F32)


def others(index, split):
    sizes = [size for size, _ in split]
    steps = list(itertools.product(*[range(size) for size in sizes]))[1:]
    steps.sort(key=lambda step: -sum(hops * min(k, size - k) for k, (size, hops) in zip(step, split)))
    found = []
    for step in steps:
        at, stride = 0, 1
        for k, size in reversed(list(zip(step, sizes))):
            digit = lax.rem(lax.div(index, jnp.int32(stride)), jnp.int32(size))
            at = at + lax.rem(digit + k, jnp.int32(size)) * stride
            stride *= size
        found.append(at)
    return found


def shift_lanes(x, by):
    return pltpu.roll(x, by % x.shape[1], 1)


def shift_rows(x, by):
    return pltpu.roll(x, by % x.shape[0], 0)


def kernel(
    nx,
    ny,
    *refs,
):
    given, refs = refs[:14], refs[14:]
    (f_out, e_out), refs = refs[:2], refs[2:]
    here, refs = refs[:14], refs[14:]
    vel, w1, b1, w2, b2, w3, b3, d1, d2, thick, eta, face, stor, ocean = here
    (
        v_rows,
        v_cols,
        v_corner,
        st_own,
        fx_own,
        fx_all,
        rv_rows,
        rv_cols,
        rv_corner,
        rst_cols,
        rst_rows,
        rfx_cols,
        rfx_rows,
        red_a,
        red_b,
        got_a,
        got_b,
        vx,
        bmat,
        pick,
        umat,
        w1pad,
        w1all,
        w2all,
        w3f,
        h1,
        mixed1,
        h2,
        zacc,
        mixed_out,
        perm,
        v_send,
        v_recv,
        s_send,
        s_recv,
        x_send,
        x_recv,
        a_send,
        a_recv,
        b_send,
        b_recv,
        load_sem,
    ) = refs
    mx = lax.axis_index("gx")
    my = lax.axis_index("gy")

    def there(step_x, step_y):
        return (lax.rem(mx + step_x + nx, nx), lax.rem(my + step_y + ny, ny))

    barrier = pltpu.get_barrier_semaphore()
    peers_x = [(at, my) for at in others(mx, SPLIT_X)]
    peers_y = [(mx, at) for at in others(my, SPLIT_Y)]
    peers = [there(sx, sy) for sx, sy in WAYS[4:]] + peers_x[::-1] + peers_y[::-1]
    loads = [pltpu.make_async_copy(src, dst, load_sem.at[n]) for n, (src, dst) in enumerate(zip(given, here))]
    loads[0].start()
    for peer in peers:
        pl.semaphore_signal(barrier, inc=1, device_id=peer, device_id_type=MESH)
    for n in LOAD_ORDER[1:]:
        loads[n].start()
    loads[0].wait()

    lane = iota((ROWS, COLS), 1)
    group = lane // 32
    low = lane % 32 < 16
    own = [[vel[l, c].astype(F32) for c in range(2)] for l in range(LEVELS)]
    for c in range(2):
        packed = None
        for l in range(LEVELS):
            first = own[l][c] if l == 0 else shift_lanes(own[l][c], 32 * l)
            last = own[l][c] if l == 3 else shift_lanes(own[l][c], 32 * (l + 1))
            both = jnp.where(low, first, last)
            packed = both if l == 0 else jnp.where(group == l, both, packed)
        v_cols[pl.ds(16 * c, 16), :] = packed.astype(BF16)
        if c == 0:
            packed_first = packed
    for side in range(2):
        cut = slice(8, 16) if side == 0 else slice(0, 8)
        rows = jnp.concatenate([own[l][c][cut] for l in range(LEVELS) for c in range(2)], axis=0)
        v_rows[side] = rows.astype(BF16)
        v_corner[side] = jnp.concatenate([packed_first[cut], packed[cut]], axis=0).astype(BF16)

    pl.semaphore_wait(barrier, len(peers))

    copies_v, copies_s = [], []
    for d in SEND_ORDER:
        sx, sy = WAYS[d]
        side = 0 if sy == 1 else 1
        if sy == 0:
            src, dst = v_cols, rv_cols.at[d]
        elif sx == 0:
            src, dst = v_rows.at[side], rv_rows.at[d - 2]
        else:
            src, dst = v_corner.at[side], rv_corner.at[d - 4]
        copy = pltpu.make_async_remote_copy(
            src_ref=src,
            dst_ref=dst,
            send_sem=v_send.at[d],
            recv_sem=v_recv.at[d],
            device_id=there(sx, sy),
            device_id_type=MESH,
        )
        copy.start()
        copies_v.append(copy)
    for n in LOAD_ORDER[5:]:
        loads[n].wait()
    w1pad[...] = jnp.zeros_like(w1pad)
    for dy in range(5):
        for dx in range(5):
            taps = w1[dy, dx].astype(F32)
            for c in range(2):
                w1pad[dx, c, pl.ds(10 + dy, 1), pl.ds(0, 128)] = taps[c : c + 1]
                w1pad[dx, c, pl.ds(11 + dy, 1), pl.ds(128, 128)] = taps[c : c + 1]
    for s in range(6):
        for dx in range(5):
            for c in range(2):
                block = w1pad[dx, c, pl.ds(10 - 2 * s, 16), :]
                w1all[s, pl.ds(32 * dx + 16 * c, 16), :] = block.astype(BF16)
        w1all[s, pl.ds(160, 96), :] = jnp.zeros((96, 256), BF16)

    kept = [d1[pl.ds(m, 1), :].astype(F32).astype(BF16) for m in range(2)]
    nothing = jnp.zeros((64, 128), BF16)
    left4 = left5 = jnp.zeros((64, 128), F32)
    for dy in range(-1, 6):
        if 0 <= dy < 5:
            g = [w2[dy, dx].astype(F32) for dx in range(5)]
            sum4 = g[0] + g[1] + left4
            sum5 = g[2] + g[3] + left5
            mixes = [g[0], g[2], g[1], g[3], g[4], sum4, sum5]
            mixes = [mix.astype(BF16) for mix in mixes]
            left4 = sum4 - mixes[5].astype(F32)
            left5 = sum5 - mixes[6].astype(F32)
        for n in range(7):
            for m in range(2):
                block = mixes[n] * kept[m] if 0 <= dy < 5 else nothing
                for b in range(2):
                    if 0 <= dy + b < 6:
                        o, a = divmod(dy + b, 2)
                        w2all[pl.ds(128 * b + 64 * m, 64), pl.ds(((n * 3 + o) * 2 + a) * 128, 128)] = block

    w3f[...] = jnp.zeros_like(w3f)
    for ky in range(3):
        for dx in range(3):
            taps = w3[ky, dx].astype(F32) * 0.5
            for c in range(2):
                tap = taps[c : c + 1]
                both = jnp.concatenate([tap, tap], axis=1)
                for b in range(2):
                    w3f[pl.ds(8 * dx + 2 * (b + 2 - ky) + c, 1), pl.ds(128 * b, 128)] = both

    r = iota((M_V, 128), 0)
    lev = (r // 4) % 4
    x = 32 * (r % 4) + r // 16 - 5
    spot = jnp.where(x < 0, 512 + 32 * lev + 32 + x, jnp.where(x < 128, 128 * lev + x, 384 + 32 * lev + x))
    for k in range(5):
        pick[:, pl.ds(128 * k, 128)] = jnp.where(iota((M_V, 128), 1) + 128 * k == spot, 1.0, 0.0).astype(BF16)
    r = iota((512, 128), 0)
    spot = 128 * ((r // 4) % 4) + 32 * (r % 4) + r // 16
    for k in range(4):
        perm[:, pl.ds(128 * k, 128)] = jnp.where(iota((512, 128), 1) + 128 * k == spot, 1.0, 0.0).astype(BF16)

    for n in LOAD_ORDER[1:5]:
        loads[n].wait()
    st_own[0] = eta[...]
    st_own[1] = face[0]
    st_own[2] = face[1]
    st_own[3] = stor[...]
    st_own[4] = ocean[...].astype(F32)
    for d in SEND_ORDER:
        sx, sy = WAYS[d]
        if sy == 0:
            src, dst = st_own, rst_cols.at[d]
        else:
            src = st_own.at[:, pl.ds(8 if sy == 1 else 0, 8), :]
            dst = rst_rows.at[d - 2]
        copy = pltpu.make_async_remote_copy(
            src_ref=src,
            dst_ref=dst,
            send_sem=s_send.at[d],
            recv_sem=s_recv.at[d],
            device_id=there(sx, sy),
            device_id_type=MESH,
        )
        copy.start()
        copies_s.append(copy)

    has_south = jnp.where(my > 0, 1.0, 0.0)
    has_north = jnp.where(my < ny - 1, 1.0, 0.0)
    for copy in copies_v:
        copy.wait_recv()
    low8 = low[:8]
    south = rv_rows[0].astype(F32) * has_south
    north = rv_rows[1].astype(F32) * has_north
    from_w, from_e = rv_cols[0].astype(F32), rv_cols[1].astype(F32)
    from_sw, from_se = rv_corner[0].astype(F32), rv_corner[1].astype(F32)
    from_nw, from_ne = rv_corner[2].astype(F32), rv_corner[3].astype(F32)
    for c in range(2):
        for l in range(LEVELS):
            at = 8 * (2 * l + c)
            vx[l, c, pl.ds(0, 8), :] = south[at : at + 8]
            vx[l, c, pl.ds(8, 16), :] = own[l][c]
            vx[l, c, pl.ds(24, 8), :] = north[at : at + 8]
        cut = slice(8 * c, 8 * c + 8)
        vx[4, c, pl.ds(0, 8), :] = jnp.where(low8, from_se[cut], from_sw[cut]) * has_south
        cut16 = slice(16 * c, 16 * c + 16)
        vx[4, c, pl.ds(8, 16), :] = jnp.where(low, from_e[cut16], from_w[cut16])
        vx[4, c, pl.ds(24, 8), :] = jnp.where(low8, from_ne[cut], from_nw[cut]) * has_north
    for w in range(2):
        for k in range(5):
            for c in range(2):
                block = vx[k, c, pl.ds(3 + 10 * w, 16), :].astype(BF16)
                for rep in range(4):
                    bmat[pl.ds(128 * w + 32 * rep + 16 * c, 16), pl.ds(128 * k, 128)] = block
    umat[...] = dot_t(pick[...], bmat[...]).astype(BF16)

    bias1 = jnp.concatenate([b1[...].reshape(1, 128)] * 2, axis=1)
    upper = iota((1, 256), 1) // 128
    group1 = iota((M_1, 128), 1) // 32
    for w in range(2):
        lanes = pl.ds(128 * w, 128)
        near = umat[pl.ds(0, M_1), lanes]
        for g in range(1, 4):
            near = jnp.where(group1 == g, umat[pl.ds(16 * g, M_1), lanes], near)
        wide = jnp.concatenate([near, umat[pl.ds(64, M_1), lanes]], axis=1)

        for j in range(6 * w, 6 + 5 * w):
            acc = dot(wide, w1all[j - 5 * w])
            row = my * ROWS + 2 * j - 3 + upper
            scale = jnp.where((row >= 0) & (row < ny * ROWS), KEEP_SCALE, 0.0)
            hidden = (jnp.maximum(acc + bias1, 0.0) * scale).astype(BF16)
            h1[j] = hidden.reshape(XO_1 // 2, 32, 256)
            d = [h1[j, pl.ds(k // 2, U_2), pl.ds(16 * (k % 2), 16), :] for k in range(5)]
            mixes = (d[0] - d[1], d[2] - d[3], d[2] - d[1], d[4] - d[3])
            for n, mix in enumerate(mixes):
                mixed1[n, j] = mix

    bias2 = jnp.concatenate([b2[...].reshape(1, 64)] * 4, axis=1)
    keep2 = d2[...].astype(F32) * KEEP_SCALE
    keep2 = jnp.concatenate([keep2[0:1], keep2[1:2]] * 2, axis=1)
    w3all = w3f[...].astype(BF16)

    def layer_two(first, spans):
        def product(*which):
            total = None
            for (n, k), o in itertools.product(which, range(3)):
                lefts = []
                for start, length in spans:
                    if k is None:
                        left = mixed1[n, pl.ds(first + o, 3), pl.ds(start, length), :, :]
                    else:
                        left = h1[pl.ds(first + o, 3), pl.ds(start + k // 2, length), pl.ds(16 * (k % 2), 16), :]
                    lefts.append(left.reshape(48 * length, 256))
                left = lefts[0] if len(lefts) == 1 else jnp.concatenate(lefts, axis=0)
                term = dot_t(left, w2all[:, pl.ds((n * 3 + o) * 256, 256)])
                total = term if total is None else total + term
            return total

        both = product((5, 1), (6, 3))
        even = product((0, None), (1, None), (4, 4)) + both
        odd = product((2, None), (3, None), (4, 5)) + both
        at = 0
        for start, length in spans:
            for q in range(3):
                row = my * ROWS + 2 * (first + q) - 1 + upper
                scale = jnp.where((row >= 0) & (row < ny * ROWS), keep2, 0.0)
                for e, acc in enumerate((even, odd)):
                    hidden = jnp.maximum(acc[at : at + 16 * length] + bias2, 0.0) * scale
                    h2[first + q, pl.ds(start, length), pl.ds(16 * e, 16), :] = hidden.astype(BF16).reshape(length, 16, 256)
                at += 16 * length

    def layer_three(first):
        for i in range(first, first + 3):
            z = dot_t(w3all, h2[i].reshape(M_2, 256))
            zacc[i] = z[0:8, 0:512] + z[8:16, 16:528] + z[16:24, 32:544]

    def finish(fx, f):
        mixed = jnp.concatenate([zacc[p, pl.ds(4, 4), :] + zacc[p + 1, pl.ds(0, 4), :] for p in range(8)], axis=0)
        high = mixed.astype(BF16)
        rest = (mixed - high.astype(F32)).astype(BF16)
        out = dot(jnp.concatenate([high, rest], axis=0), perm[...])
        for l in range(LEVELS):
            lanes = slice(128 * l, 128 * l + 128)
            mixed_out[l] = out[0:32, lanes] + out[32:64, lanes]
        for c in range(2):
            total = None
            for l in range(LEVELS):
                forcing = mixed_out[l, pl.ds(c, 16, stride=2), :] + b3[c]
                if f is not None:
                    f[l, c] = forcing
                term = thick[l] * (vel[l, c].astype(F32) + forcing)
                total = term if total is None else total + term
            fx[c] = total

    layer_two(0, [(0, U_2)])
    layer_two(6, [(0, U_2)])
    h2[pl.ds(3, 3), pl.ds(EDGE_W, EDGE_E - EDGE_W), :, :] = jnp.zeros((3, EDGE_E - EDGE_W, 32, 256), BF16)
    layer_two(3, [(0, EDGE_W), (EDGE_E, U_2 - EDGE_E)])
    layer_three(0)
    layer_three(6)
    layer_three(3)
    finish(fx_own, None)

    copies_x = []
    for d in SEND_ORDER:
        sx, sy = WAYS[d]
        if sy == 0:
            src, dst = fx_own, rfx_cols.at[d]
        else:
            src = fx_own.at[:, pl.ds(8 if sy == 1 else 0, 8), :]
            dst = rfx_rows.at[d - 2]
        copy = pltpu.make_async_remote_copy(
            src_ref=src,
            dst_ref=dst,
            send_sem=x_send.at[d],
            recv_sem=x_recv.at[d],
            device_id=there(sx, sy),
            device_id_type=MESH,
        )
        copy.start()
        copies_x.append(copy)

    layer_two(3, [(EDGE_W, EDGE_E - EDGE_W)])
    layer_three(3)
    finish(fx_all, f_out)

    for copy in copies_s:
        copy.wait_recv()

    side = iota((ROWS, COLS), 1) < 64
    side8 = side[:8]

    def widened(own_ref, cols_ref, rows_ref, k):
        middle = jnp.concatenate([own_ref[k], jnp.where(side, cols_ref[1, k], cols_ref[0, k])], axis=1)
        below = jnp.concatenate([rows_ref[0, k], jnp.where(side8, rows_ref[3, k], rows_ref[2, k])], axis=1)
        above = jnp.concatenate([rows_ref[1, k], jnp.where(side8, rows_ref[5, k], rows_ref[4, k])], axis=1)
        return jnp.concatenate([below, middle, above], axis=0)

    eta_w, east_w, north_w, stor_w, sea = [widened(st_own, rst_cols, rst_rows, k) for k in range(5)]
    place = iota(sea.shape, 0) - 8 + my * ROWS
    sea = jnp.where((place >= 0) & (place < ny * ROWS), sea, 0.0)
    open_east = sea * shift_lanes(sea, -1)
    open_north = sea * shift_rows(sea, -1)
    coef_east = east_w * open_east
    coef_north = north_w * open_north
    coef_west = shift_lanes(coef_east, 1)
    coef_south = shift_rows(coef_north, 1)
    diagonal = stor_w + coef_east + coef_west + coef_north + coef_south

    def operate(field):
        return (
            diagonal * field
            - coef_east * shift_lanes(field, -1)
            - coef_west * shift_lanes(field, 1)
            - coef_north * shift_rows(field, -1)
            - coef_south * shift_rows(field, 1)
        )

    known = stor_w * eta_w - operate(eta_w)
    for copy in copies_x:
        copy.wait_recv()
    zonal, merid = [widened(fx_all, rfx_cols, rfx_rows, k) for k in range(2)]
    flux_east = zonal * open_east
    flux_north = merid * open_north
    diverge = flux_east - shift_lanes(flux_east, 1) + flux_north - shift_rows(flux_north, 1)
    k0 = known - diverge
    k1 = operate(k0)
    k2 = operate(k1)
    k3 = operate(k2)
    k0, k1, k2, k3 = [k[8:24, 0:128] for k in (k0, k1, k2, k3)]

    lane1 = iota((1, 128), 1)
    sums = jnp.zeros((1, 128), F32)
    for n, (a, b) in enumerate(((k0, k0), (k0, k1), (k1, k1), (k1, k2), (k2, k2), (k2, k3))):
        total = jnp.sum(jnp.sum(a * b, axis=0, keepdims=True), axis=1, keepdims=True)
        sums = jnp.where(lane1 == n, total, sums)

    def exchange(values, mine, got, send, recv, targets):
        mine[...] = values
        copies = []
        for k, target in enumerate(targets):
            copy = pltpu.make_async_remote_copy(
                src_ref=mine,
                dst_ref=got.at[k],
                send_sem=send.at[k],
                recv_sem=recv.at[k],
                device_id=target,
                device_id_type=MESH,
            )
            copy.start()
            copies.append(copy)
        for copy in copies:
            copy.wait_recv()
        return values + jnp.sum(got[...], axis=0), copies

    sums, copies_a = exchange(sums, red_a, got_a, a_send, a_recv, peers_x)
    sums, copies_b = exchange(sums, red_b, got_b, b_send, b_recv, peers_y)
    m0, m1, m2, m3, m4, m5 = [
        jnp.sum(jnp.where(lane1 == n, sums, 0.0), axis=1, keepdims=True) for n in range(6)
    ]

    def over(value, scale):
        fine = value > 1e-6 * scale
        return jnp.where(fine, 1.0 / jnp.where(fine, value, 1.0), 0.0)

    inv0 = over(m1, jnp.zeros_like(m1))
    l1 = m2 * inv0
    l2 = m3 * inv0
    p1 = m3 - l1 * m2
    inv1 = over(p1, m3)
    e21 = m4 - l2 * m2
    l21 = e21 * inv1
    p2 = m5 - l2 * m3 - l21 * e21
    inv2 = jnp.where(inv1 > 0.0, over(p2, m5), 0.0)
    z1 = m1 - l1 * m0
    z2 = m2 - l2 * m0 - l21 * z1
    c2 = z2 * inv2
    c1 = z1 * inv1 - l21 * c2
    c0 = m0 * inv0 - l1 * c1 - l2 * c2
    e_out[...] = eta[...] + c0 * k0 + c1 * k1 + c2 * k2

    for copy in copies_v + copies_s + copies_x + copies_a + copies_b:
        copy.wait_send()


def body(nx, ny, *args):
    vmem = pl.BlockSpec(memory_space=pltpu.VMEM)
    args = list(args)
    args[1] = jnp.transpose(args[1], (1, 2, 0, 3))
    args[5] = jnp.transpose(args[5], (1, 2, 0, 3))
    here = [(pltpu.SMEM if n in (6, 9) else pltpu.VMEM)(a.shape, a.dtype) for n, a in enumerate(args)]
    dma = pltpu.SemaphoreType.DMA
    V = pltpu.VMEM
    return pl.pallas_call(
        functools.partial(kernel, nx, ny),
        out_shape=(
            pltpu.VMEM((LEVELS, 2, ROWS, COLS), F32),
            pltpu.VMEM((ROWS, COLS), F32),
        ),
        in_specs=[pl.BlockSpec(memory_space=pltpu.HBM)] * 14,
        out_specs=(vmem, vmem),
        scratch_shapes=here + [
            V((2, 64, 128), BF16),
            V((32, 128), BF16),
            V((2, 16, 128), BF16),
            V((5, ROWS, COLS), F32),
            V((2, ROWS, COLS), F32),
            V((2, ROWS, COLS), F32),
            V((2, 64, 128), BF16),
            V((2, 32, 128), BF16),
            V((4, 16, 128), BF16),
            V((2, 5, ROWS, COLS), F32),
            V((6, 5, 8, COLS), F32),
            V((2, 2, ROWS, COLS), F32),
            V((6, 2, 8, COLS), F32),
            V((1, 128), F32),
            V((1, 128), F32),
            V((nx - 1, 1, 128), F32),
            V((ny - 1, 1, 128), F32),
            V((5, 2, 32, 128), F32),
            V((256, 640), BF16),
            V((M_V, 640), BF16),
            V((M_V, 256), BF16),
            V((5, 2, 32, 256), F32),
            V((6, 256, 256), BF16),
            V((256, 7 * 768), BF16),
            V((32, 256), F32),
            V((11, XO_1 // 2, 32, 256), BF16),
            V((4, 11, U_2, 16, 256), BF16),
            V((9, U_2, 32, 256), BF16),
            V((9, 8, 512), F32),
            V((LEVELS, 32, 128), F32),
            V((512, 512), BF16),
            dma((8,)),
            dma((8,)),
            dma((8,)),
            dma((8,)),
            dma((8,)),
            dma((8,)),
            dma((nx - 1,)),
            dma((nx - 1,)),
            dma((ny - 1,)),
            dma((ny - 1,)),
            dma((14,)),
        ],
        compiler_params=pltpu.CompilerParams(
            collective_id=0, has_side_effects=True, vmem_limit_bytes=60 * 2**20
        ),
        name="ocean_step",
    )(*args)


def solution(mesh):
    nx, ny = mesh.shape["gx"], mesh.shape["gy"]
    tile = P("gy", "gx")
    stacked = P(None, "gy", "gx")
    levels = P(None, None, "gy", "gx")
    in_specs = (levels,) + (P(),) * 9 + (tile, stacked, tile, tile)
    return jax.shard_map(
        functools.partial(body, nx, ny),
        mesh=mesh,
        in_specs=in_specs,
        out_specs=(levels, tile),
        check_vma=False,
    )
```
